128 devices in a mesh: gx: 16 (over z, y), gy: 8 (over x, core).
Axes of the slice: x: 4, y: 4, z: 4, core: 2. Of those that a mesh axis runs over, the one named last changes fastest.
Arguments:
- right_side: float32 [2, 3, 8, 256, 1024], P(None, None, None, 'gx', 'gy'), may hold values from -20 to 20
- conductivity: float32 [3, 8, 256, 1024], P(None, None, 'gx', 'gy'), may hold values from 0 to 8
- bloch_index: int32 [2], replicated, may hold values from 1 to 15
Outputs:
- solution: float32 [2, 3, 8, 256, 1024], P(None, None, None, 'gx', 'gy')
- residual: float32 [2, 3, 8, 256, 1024], P(None, None, None, 'gx', 'gy')
The draws below stay inside these ranges and needn't reach their ends.
All inputs are finite; a program needn't handle non-finite values.
Results may differ from the reference program's by a relative error of at most 0.00045.
Values sent between devices are 32-bit elements; how exact they have to be, the bound alone decides.
No kernel may reach another device: no remote copies, remote signals or barrier semaphores. Data moves between devices by JAX's collectives and lax.ppermute only.
A program may use at most 128 MiB of HBM per device.

```python
import math
import jax
import jax.numpy as jnp
from jax import lax

S = 4
OUTER = 3
NZ = 8
NX = 256
NY = 1024


def lateral_distance(center, length):
    spots = jnp.arange(length, dtype=jnp.int32)
    ahead = (spots - center) % length
    return jnp.minimum(ahead, length - ahead).astype(jnp.float32)


def draw_right_side(key, part):
    key = jax.random.fold_in(key, 23)
    center_key, noise_key = jax.random.split(key)
    center_x = jax.random.randint(jax.random.fold_in(center_key, 1), (), 0, NX)
    center_y = jax.random.randint(jax.random.fold_in(center_key, 2), (), 0, NY)
    reach_x = lateral_distance(center_x, NX)
    reach_y = lateral_distance(center_y, NY)
    dist_x = reach_x / (0.25 * NX)
    dist_y = reach_y / (0.25 * NY)
    bump = jnp.exp(-0.5 * (dist_x[:, None] * dist_x[:, None] + dist_y[None, :] * dist_y[None, :]))
    amplitude = 0.5 * jnp.power(10.0, bump)
    shape = (2, 3, NZ, NX, NY)
    base = jax.random.truncated_normal(noise_key, -4.0, 4.0, shape, jnp.float32)
    return (amplitude * base).astype(jnp.float32)


def draw_conductivity(key, part):
    key = jax.random.fold_in(key, 11)
    start_key, value_key = jax.random.split(key)
    start_x = jax.random.randint(jax.random.fold_in(start_key, 1), (), 0, NX)
    start_y = jax.random.randint(jax.random.fold_in(start_key, 2), (), 0, NY)
    inside_x = (jnp.arange(NX, dtype=jnp.int32) - start_x) % NX < NX // 2
    inside_y = (jnp.arange(NY, dtype=jnp.int32) - start_y) % NY < NY // 2
    layers = jnp.arange(NZ, dtype=jnp.int32)
    inside_z = (layers >= NZ // 4) & (layers < NZ // 4 + max(NZ // 2, 1))
    inside = inside_z[:, None, None] & inside_x[None, :, None] & inside_y[None, None, :]
    shape = (3, NZ, NX, NY)
    values = jnp.exp(jax.random.uniform(value_key, shape, jnp.float32, math.log(0.5), math.log(8.0)))
    return jnp.where(inside[None], values, 0.0).astype(jnp.float32)


def setup_inputs(seed: int = 0) -> dict:
    splits = jax.random.split(jax.random.key(seed), 4)
    return {
        "right_side": draw_right_side(jax.random.fold_in(splits[3], 71), 0),
        "conductivity": draw_conductivity(jax.random.fold_in(splits[3], 71), 0),
        "bloch_index": jax.random.randint(splits[2], (2,), 1, 16).astype(jnp.int32),
    }


shift_real = 0.5
level_step = 0.4
basis_scale = 16.0
ridge_share = 0.001
bloch_steps = 16.0

def rotate(field, cosine, sine):
    return jnp.stack([field[0] * cosine - field[1] * sine, field[0] * sine + field[1] * cosine])

def zahead(field):
    return jnp.concatenate([field[..., 1:, :, :], jnp.zeros_like(field[..., :1, :, :])], axis=-3)

def zbehind(field):
    return jnp.concatenate([jnp.zeros_like(field[..., :1, :, :]), field[..., :-1, :, :]], axis=-3)

def curl_curl(field):
    edge_x, edge_y, edge_z = (field[:, 0], field[:, 1], field[:, 2])

    def ahead_x(part):
        return part[..., 1:, :-1] - part[..., :-1, :-1]

    def ahead_y(part):
        return part[..., :-1, 1:] - part[..., :-1, :-1]

    def ahead_z(part):
        center = part[..., :-1, :-1]
        return zahead(center) - center
    curl_x = ahead_y(edge_z) - ahead_z(edge_y)
    curl_y = ahead_z(edge_x) - ahead_x(edge_z)
    curl_z = ahead_x(edge_y) - ahead_y(edge_x)

    def back_x(part):
        return part[..., :-1, 1:] - part[..., 1:, 1:]

    def back_y(part):
        return part[..., 1:, :-1] - part[..., 1:, 1:]

    def back_z(part):
        center = part[..., 1:, 1:]
        return zbehind(center) - center
    out_x = back_z(curl_y) - back_y(curl_z)
    out_y = back_x(curl_z) - back_z(curl_x)
    out_z = back_y(curl_x) - back_x(curl_y)
    return jnp.stack([out_x, out_y, out_z], axis=1)

def apply_operator(padded, conductivity):
    center = padded[..., 1:-1, 1:-1]
    swirl = curl_curl(padded)
    scaled = level_step * conductivity.astype(jnp.float32)
    real_part = swirl[0] + shift_real * center[0] - scaled * center[1]
    imag_part = swirl[1] + shift_real * center[1] + scaled * center[0]
    return jnp.stack([real_part, imag_part]) / basis_scale

def bloch_pad(field, theta_x, theta_y):
    low_x = rotate(field[..., -1:, :], jnp.cos(theta_x), -jnp.sin(theta_x))
    high_x = rotate(field[..., :1, :], jnp.cos(theta_x), jnp.sin(theta_x))
    wider = jnp.concatenate([low_x, field, high_x], axis=3)
    low_y = rotate(wider[..., -1:], jnp.cos(theta_y), -jnp.sin(theta_y))
    high_y = rotate(wider[..., :1], jnp.cos(theta_y), jnp.sin(theta_y))
    return jnp.concatenate([low_y, wider, high_y], axis=4)

def gram_matrix(basis):
    stacked = jnp.stack(basis).reshape(len(basis), 2, -1)
    real_rows, imag_rows = (stacked[:, 0], stacked[:, 1])
    highest = lax.Precision.HIGHEST
    gram_real = jnp.dot(real_rows, real_rows.T, precision=highest) + jnp.dot(imag_rows, imag_rows.T, precision=highest)
    gram_imag = jnp.dot(real_rows, imag_rows.T, precision=highest) - jnp.dot(imag_rows, real_rows.T, precision=highest)
    return (gram_real, gram_imag)

def coefficients(gram_real, gram_imag):
    herm_real = basis_scale * basis_scale * gram_real[1:, 1:]
    herm_imag = basis_scale * basis_scale * gram_imag[1:, 1:]
    load_real = basis_scale * gram_real[1:, 0]
    load_imag = basis_scale * gram_imag[1:, 0]
    count = herm_real.shape[0]
    shift_diag = ridge_share * jnp.trace(herm_real) / count * jnp.eye(count, dtype=herm_real.dtype)
    system = jnp.concatenate([jnp.concatenate([herm_real + shift_diag, -herm_imag], axis=1), jnp.concatenate([herm_imag, herm_real + shift_diag], axis=1)], axis=0)
    target = jnp.concatenate([load_real, load_imag])
    factor = jnp.linalg.cholesky(system)
    answer = jax.scipy.linalg.cho_solve((factor, True), target)
    return (answer[:count], answer[count:])

def combine(vectors, coef_real, coef_imag):
    summed = rotate(vectors[0], coef_real[0], coef_imag[0])
    for index in range(1, len(vectors)):
        summed = summed + rotate(vectors[index], coef_real[index], coef_imag[index])
    return summed

def reference(right_side, conductivity, bloch_index):
    theta = 2.0 * math.pi * bloch_index.astype(jnp.float32) / bloch_steps
    theta_x, theta_y = (theta[0], theta[1])
    solution = jnp.zeros_like(right_side)
    residual = right_side
    for sweep in range(OUTER):
        basis = [residual]
        current = residual
        for power in range(S):
            current = apply_operator(bloch_pad(current, theta_x, theta_y), conductivity)
            basis.append(current)
        gram_real, gram_imag = gram_matrix(basis)
        coef_real, coef_imag = coefficients(gram_real, gram_imag)
        solution = solution + combine(basis[:S], coef_real, coef_imag)
        residual = residual - basis_scale * combine(basis[1:], coef_real, coef_imag)
    return (solution, residual)
```

```python
import functools
import math

import jax
import jax.numpy as jnp
from jax import lax
from jax.experimental import pallas as pl
from jax.experimental.pallas import tpu as pltpu
from jax.sharding import PartitionSpec as P

S = 4
NZ = 8
ROWS = 16
LANES = 128
WIDE = 48
MID = 32
SPAN = 256

shift_real = 0.5
level_step = 0.4
basis_scale = 16.0
ridge_share = 0.001
bloch_steps = 16.0

VMEM = pl.BlockSpec(memory_space=pltpu.VMEM)
SMEM = pl.BlockSpec(memory_space=pltpu.SMEM)
LIMIT = 16 * 1024 * 1024
PAIRS = [(j, k) for j in range(S + 1) for k in range(j, S + 1) if k > 0]


def lane_index(rows):
    return lax.broadcasted_iota(jnp.int32, (rows, LANES), 1)


def sub_index(rows):
    return lax.broadcasted_iota(jnp.int32, (rows, LANES), 0)


def pack_kernel(rs_ref, cond_ref, last_ref, first_ref, left_ref, right_ref):
    lanes = lane_index(ROWS)
    subs = sub_index(8)

    def pack(source, offset):
        def body(group, _):
            left = jnp.zeros((ROWS, LANES), jnp.float32)
            right = jnp.zeros((ROWS, LANES), jnp.float32)
            low, high = None, None
            for spot in range(8):
                plane = source[(group - offset) * 8 + spot]
                top, bottom = plane[:8], plane[8:]
                last_ref[group * 8 + spot] = bottom
                first_ref[group * 8 + spot] = top
                if spot % 2 == 0:
                    low, high = top, bottom
                else:
                    half = 72 + group * 4 + spot // 2
                    last_ref[half] = jnp.where(subs < 4, pltpu.roll(low, 4, 0), top)
                    first_ref[half] = jnp.where(subs < 4, high, pltpu.roll(bottom, 4, 0))
                inside = (lanes >= 16 * spot) & (lanes < 16 * spot + 16)
                ahead = pltpu.roll(plane, (16 * spot + 16) % LANES, 1)
                behind = plane if spot == 0 else pltpu.roll(plane, 16 * spot, 1)
                right = jnp.where(inside, ahead, right)
                left = jnp.where(inside, behind, left)
            left_ref[group] = left
            right_ref[group] = right
            return 0

        return body

    lax.fori_loop(0, 6, pack(rs_ref, 0), 0)
    lax.fori_loop(6, 9, pack(cond_ref, 6), 0)


def pack_messages(right_side, conductivity):
    lines = jax.ShapeDtypeStruct((108, 8, LANES), jnp.float32)
    strips = jax.ShapeDtypeStruct((9, ROWS, LANES), jnp.float32)
    return pl.pallas_call(
        pack_kernel,
        out_shape=(lines, lines, strips, strips),
        in_specs=[VMEM, VMEM],
        out_specs=(VMEM,) * 4,
        compiler_params=pltpu.CompilerParams(vmem_limit_bytes=LIMIT),
        name="pack_messages",
    )(right_side.reshape(48, ROWS, LANES), conductivity.reshape(24, ROWS, LANES))


def turn(real, imag, cosine, sine):
    return real * cosine - imag * sine, real * sine + imag * cosine


def fill(scal_ref, rs_ref, cond_ref, last_ref, first_ref, sides_ref, above_ref, below_ref, basis_ref, sigma_ref):
    lanes16 = lane_index(ROWS)
    lanes = lane_index(1)
    cos_b = jnp.where(lanes < 64, scal_ref[6], scal_ref[4])
    sin_b = jnp.where(lanes < 64, scal_ref[7], scal_ref[5])
    low_c, low_s, high_c, high_s = (scal_ref[k] for k in range(4))

    def strip(ref, group, spot):
        left, right = ref[group], ref[9 + group]
        left = pltpu.roll(left, (112 - 16 * spot) % LANES, 1) if spot != 7 else left
        right = pltpu.roll(right, (128 - 16 * spot) % LANES, 1) if spot else right
        return jnp.where(lanes16 < 64, right, left)

    def column(group, spot):
        return jnp.concatenate(
            [strip(above_ref, group, spot), strip(sides_ref, group, spot), strip(below_ref, group, spot)], axis=0
        )

    def lines(source, group, base, spot):
        subs = sub_index(8)
        plane = group * 8 + spot
        half = 72 + group * 4 + spot // 2
        before, after = last_ref[half], first_ref[half]
        if spot % 2 == 0:
            before = pltpu.roll(before, 4, 0)
        else:
            after = pltpu.roll(after, 4, 0)
        zero = jnp.zeros((8, LANES), jnp.float32)
        before = jnp.where(subs < 4, zero, before)
        after = jnp.where(subs < 4, after, zero)
        return jnp.concatenate(
            [before, last_ref[plane], source[(group - base) * 8 + spot], first_ref[plane], after], axis=0
        )

    def body(comp, _):
        for spot in range(NZ):
            real, imag = lines(rs_ref, comp, 0, spot), lines(rs_ref, comp + 3, 0, spot)
            real_b, imag_b = column(comp, spot), column(comp + 3, spot)
            real_b, imag_b = turn(real_b, imag_b, cos_b, sin_b)
            for part, at in ((real, imag), 0), ((real_b, imag_b), LANES):
                a, b = part
                lo = turn(a[:16], b[:16], low_c, low_s)
                hi = turn(a[32:], b[32:], high_c, high_s)
                for ri, whole in enumerate((a, b)):
                    basis_ref[0, ri, comp, spot, 0:16, at : at + LANES] = lo[ri]
                    basis_ref[0, ri, comp, spot, 16:32, at : at + LANES] = whole[16:32]
                    basis_ref[0, ri, comp, spot, 32:48, at : at + LANES] = hi[ri]
            sigma = lines(cond_ref, comp + 6, 6, spot)
            sigma_b = column(comp + 6, spot)
            factor = level_step / basis_scale
            sigma_ref[comp, spot, :, 0:LANES] = sigma * factor
            sigma_ref[comp, spot, :, LANES:SPAN] = sigma_b * factor
        return 0

    lax.fori_loop(0, 3, body, 0)


def apply_step(basis_ref, sigma_ref, k, rows, sigma_row):
    inverse = 1.0 / basis_scale

    def ahead_x(v):
        return pltpu.roll(v, rows - 1, 0) - v

    def back_x(v):
        return pltpu.roll(v, 1, 0) - v

    def ahead_y(v):
        return pltpu.roll(v, SPAN - 1, 1) - v

    def back_y(v):
        return pltpu.roll(v, 1, 1) - v

    def body(z, carry):
        fresh, outs = [], []
        for ri in range(2):
            ex, ey, ez = (basis_ref[k, ri, c, z] for c in range(3))
            hx = ahead_y(ez) - (basis_ref[k, ri, 1, z + 1] - ey)
            hy = (basis_ref[k, ri, 0, z + 1] - ex) - ahead_x(ez)
            hz = ahead_x(ey) - ahead_y(ex)
            old_x, old_y = carry[2 * ri], carry[2 * ri + 1]
            outs.append(
                ((old_y - hy) - back_y(hz), back_x(hz) - (old_x - hx), back_y(hx) - back_x(hy))
            )
            fresh += [hx, hy]
        for c in range(3):
            real, imag = basis_ref[k, 0, c, z], basis_ref[k, 1, c, z]
            sigma = sigma_ref[c, z, sigma_row : sigma_row + rows, :]
            basis_ref[k + 1, 0, c, z] = (outs[0][c] + shift_real * real) * inverse - sigma * imag
            basis_ref[k + 1, 1, c, z] = (outs[1][c] + shift_real * imag) * inverse + sigma * real
        return tuple(fresh)

    zero = jnp.zeros((rows, SPAN), jnp.float32)
    lax.fori_loop(0, NZ, body, (zero,) * 4)


def clear_end(basis_ref, rows):
    for k in range(S):
        for ri in range(2):
            for c in range(2):
                basis_ref[k, ri, c, NZ] = jnp.zeros((rows, SPAN), jnp.float32)


def gram(basis_ref, row, sums_ref, gram_ref):
    def body(plane, sums):
        c, z = plane // NZ, plane % NZ
        for top in range(row, row + ROWS, 8):
            vs = [[basis_ref[k, ri, c, z, top : top + 8, 0:LANES] for ri in range(2)] for k in range(S + 1)]
            fresh, at = [], 0
            for j, k in PAIRS:
                fresh.append(sums[at] + (vs[j][0] * vs[k][0] + vs[j][1] * vs[k][1]))
                at += 1
            for j, k in PAIRS:
                if j != k:
                    fresh.append(sums[at] + (vs[j][0] * vs[k][1] - vs[j][1] * vs[k][0]))
                    at += 1
            sums = tuple(fresh)
        return sums

    count = len(PAIRS) + sum(j != k for j, k in PAIRS)
    sums = lax.fori_loop(0, 3 * NZ, body, (jnp.zeros((8, LANES), jnp.float32),) * count)
    sums_ref[...] = jnp.zeros((LANES, LANES), jnp.float32)
    for at, total in enumerate(sums):
        sums_ref[at : at + 1, :] = jnp.sum(total, axis=0, keepdims=True)
    gram_ref[...] = lax.dot_general(
        jnp.ones(gram_ref.shape, jnp.float32),
        sums_ref[...],
        (((1,), (1,)), ((), ())),
        precision=lax.Precision.HIGHEST,
        preferred_element_type=jnp.float32,
    )


def cmul(a, b):
    return a[0] * b[0] - a[1] * b[1], a[0] * b[1] + a[1] * b[0]


def csub(a, b):
    return a[0] - b[0], a[1] - b[1]


def conj(a):
    return a[0], -a[1]


def coefficients(gathered_ref):
    row = jnp.broadcast_to(jnp.sum(gathered_ref[...], axis=0, keepdims=True), (8, LANES))

    def pick(at):
        return jnp.broadcast_to(row[:, at : at + 1], (8, LANES))

    entry, at = {}, len(PAIRS)
    for index, (j, k) in enumerate(PAIRS):
        if j == k:
            entry[j, k] = (pick(index), None)
        else:
            entry[j, k] = (pick(index), pick(at))
            at += 1
    square = basis_scale * basis_scale
    diag = [entry[k + 1, k + 1][0] * square for k in range(S)]
    extra = (ridge_share / S) * ((diag[0] + diag[1]) + (diag[2] + diag[3]))
    diag = [d + extra for d in diag]
    low = {}
    for j in range(S):
        for k in range(j + 1, S):
            real, imag = entry[j + 1, k + 1]
            low[k, j] = (real * square, -imag * square)
    load = [(entry[0, k + 1][0] * basis_scale, -entry[0, k + 1][1] * basis_scale) for k in range(S)]
    inverse, unit = [], {}
    for k in range(S):
        inverse.append(1.0 / diag[k])
        for i in range(k + 1, S):
            unit[i, k] = (low[i, k][0] * inverse[k], low[i, k][1] * inverse[k])
        for i in range(k + 1, S):
            real, imag = low[i, k]
            diag[i] = diag[i] - (real * real + imag * imag) * inverse[k]
            for j in range(k + 1, i):
                low[i, j] = csub(low[i, j], cmul(unit[i, k], conj(low[j, k])))
            load[i] = csub(load[i], cmul(unit[i, k], load[k]))
    answer = [None] * S
    for k in reversed(range(S)):
        value = (load[k][0] * inverse[k], load[k][1] * inverse[k])
        for j in range(k + 1, S):
            value = csub(value, cmul(conj(unit[j, k]), answer[j]))
        answer[k] = value
    return [(real[0, 0], imag[0, 0]) for real, imag in answer]


def new_residual(basis_ref, coefs, c, z, window):
    real, imag = basis_ref[(0, 0, c, z) + window], basis_ref[(0, 1, c, z) + window]
    for k in range(S):
        cr, ci = coefs[k][0] * basis_scale, coefs[k][1] * basis_scale
        vr, vi = basis_ref[(k + 1, 0, c, z) + window], basis_ref[(k + 1, 1, c, z) + window]
        real = real - (vr * cr - vi * ci)
        imag = imag - (vr * ci + vi * cr)
    return real, imag


def solution_part(basis_ref, coefs, c, z, window):
    total = None
    for k in range(S):
        vr, vi = basis_ref[(k, 0, c, z) + window], basis_ref[(k, 1, c, z) + window]
        part = turn(vr, vi, coefs[k][0], coefs[k][1])
        total = part if total is None else (total[0] + part[0], total[1] + part[1])
    return total


def first_kernel(
    scal_ref, rs_ref, cond_ref, last_ref, first_ref, sides_ref, above_ref, below_ref,
    basis_ref, sigma_ref, gram_ref, sums_ref,
):
    clear_end(basis_ref, WIDE)
    fill(scal_ref, rs_ref, cond_ref, last_ref, first_ref, sides_ref, above_ref, below_ref, basis_ref, sigma_ref)
    for k in range(S):
        apply_step(basis_ref, sigma_ref, k, WIDE, 0)
    gram(basis_ref, 16, sums_ref, gram_ref)


def next_kernel(first, gathered_ref, old_ref, sigma_ref, *refs):
    if first:
        basis_ref, part_ref, gram_ref, sums_ref = refs
        old_part = None
    else:
        old_part, basis_ref, part_ref, gram_ref, sums_ref = refs
    skip = (WIDE - MID) // 2 if first else 0
    coefs = coefficients(gathered_ref)
    clear_end(basis_ref, MID)

    def body(plane, _):
        c, z = plane // NZ, plane % NZ
        for top in range(0, MID, 8):
            for at in range(0, SPAN, LANES):
                window = (slice(skip + top, skip + top + 8), slice(at, at + LANES))
                real, imag = new_residual(old_ref, coefs, c, z, window)
                basis_ref[0, 0, c, z, top : top + 8, at : at + LANES] = real
                basis_ref[0, 1, c, z, top : top + 8, at : at + LANES] = imag
                if at == 0 and 8 <= top < 24:
                    part = solution_part(old_ref, coefs, c, z, window)
                    for ri in range(2):
                        value = part[ri]
                        if old_part is not None:
                            value = value + old_part[ri, c, z, top - 8 : top, :]
                        part_ref[ri, c, z, top - 8 : top, :] = value
        return 0

    lax.fori_loop(0, 3 * NZ, body, 0)
    for k in range(S):
        apply_step(basis_ref, sigma_ref, k, MID, (WIDE - MID) // 2)
    gram(basis_ref, 8, sums_ref, gram_ref)


def last_kernel(gathered_ref, old_ref, old_part, part_ref, residual_ref):
    coefs = coefficients(gathered_ref)

    def body(plane, _):
        c, z = plane // NZ, plane % NZ
        for top in range(0, ROWS, 8):
            window = (slice(8 + top, 16 + top), slice(0, LANES))
            residual = new_residual(old_ref, coefs, c, z, window)
            part = solution_part(old_ref, coefs, c, z, window)
            for ri in range(2):
                residual_ref[ri, c, z, top : top + 8, :] = residual[ri]
                part_ref[ri, c, z, top : top + 8, :] = part[ri] + old_part[ri, c, z, top : top + 8, :]
        return 0

    lax.fori_loop(0, 3 * NZ, body, 0)


def vmem(shape):
    return pltpu.VMEM(shape, jnp.float32)


PART = (2, 3, NZ, ROWS, LANES)


def run_first(peers, scal, right_side, conductivity, last, first, sides, above, below):
    return pl.pallas_call(
        first_kernel,
        out_shape=(vmem((S + 1, 2, 3, NZ + 1, WIDE, SPAN)), vmem((3, NZ, WIDE, SPAN)), jax.ShapeDtypeStruct((peers, LANES), jnp.float32)),
        in_specs=[SMEM] + [VMEM] * 7,
        out_specs=(VMEM,) * 3,
        scratch_shapes=[vmem((LANES, LANES))],
        compiler_params=pltpu.CompilerParams(vmem_limit_bytes=LIMIT),
        name="first_sweep",
    )(scal, right_side.reshape(48, ROWS, LANES), conductivity.reshape(24, ROWS, LANES), last, first, sides, above, below)


def run_next(peers, is_first, gathered, old, sigma, *part):
    return pl.pallas_call(
        functools.partial(next_kernel, is_first),
        out_shape=(vmem((S + 1, 2, 3, NZ + 1, MID, SPAN)), vmem(PART), jax.ShapeDtypeStruct((peers, LANES), jnp.float32)),
        in_specs=[VMEM] * (3 + len(part)),
        out_specs=(VMEM,) * 3,
        scratch_shapes=[vmem((LANES, LANES))],
        compiler_params=pltpu.CompilerParams(vmem_limit_bytes=LIMIT),
        name="second_sweep" if is_first else "third_sweep",
    )(gathered, old, sigma, *part)


def run_last(gathered, old, part):
    shape = jax.ShapeDtypeStruct(PART, jnp.float32)
    return pl.pallas_call(
        last_kernel,
        out_shape=(shape, shape),
        in_specs=[VMEM] * 3,
        out_specs=(VMEM,) * 2,
        compiler_params=pltpu.CompilerParams(vmem_limit_bytes=LIMIT),
        name="last_update",
    )(gathered, old, part)


def spread(partial):
    return lax.all_to_all(partial, ("gx", "gy"), 0, 0, tiled=True)


def phases(bloch_index):
    theta = 2.0 * math.pi * bloch_index.astype(jnp.float32) / bloch_steps
    rows = []
    for axis, angle in (("gx", theta[0]), ("gy", theta[1])):
        spot, peers = lax.axis_index(axis), lax.axis_size(axis)
        cosine, sine = jnp.cos(angle), jnp.sin(angle)
        rows += [jnp.where(spot == 0, cosine, 1.0), jnp.where(spot == 0, -sine, 0.0)]
        rows += [jnp.where(spot == peers - 1, cosine, 1.0), jnp.where(spot == peers - 1, sine, 0.0)]
    return jnp.stack(rows)


def ring(axis, step):
    peers = lax.axis_size(axis)
    return [(i, (i + step) % peers) for i in range(peers)]


def shards(right_side, conductivity, bloch_index):
    peers = lax.axis_size("gx") * lax.axis_size("gy")
    scal = phases(bloch_index)
    last, first, left, right = pack_messages(right_side, conductivity)
    above = lax.ppermute(last, "gx", ring("gx", 1))
    below = lax.ppermute(first, "gx", ring("gx", -1))
    before = lax.ppermute(right, "gy", ring("gy", 1))
    after = lax.ppermute(left, "gy", ring("gy", -1))
    sides = jnp.concatenate([before, after])
    corners_above = lax.ppermute(sides, "gx", ring("gx", 1))
    corners_below = lax.ppermute(sides, "gx", ring("gx", -1))
    basis, sigma, partial = run_first(
        peers, scal, right_side, conductivity, above, below, sides, corners_above, corners_below
    )
    basis, part, partial = run_next(peers, True, spread(partial), basis, sigma)
    basis, part, partial = run_next(peers, False, spread(partial), basis, sigma, part)
    return run_last(spread(partial), basis, part)


def solution(mesh):
    in_specs = (P(None, None, None, "gx", "gy"), P(None, None, "gx", "gy"), P())
    out_specs = (P(None, None, None, "gx", "gy"), P(None, None, None, "gx", "gy"))
    return jax.shard_map(shards, mesh=mesh, in_specs=in_specs, out_specs=out_specs, check_vma=False)
```

```python
import functools
import math

import jax
import jax.numpy as jnp
from jax import lax
from jax.experimental import pallas as pl
from jax.experimental.pallas import tpu as pltpu
from jax.sharding import PartitionSpec as P

S = 4
NZ = 8
ROWS = 16
LANES = 128
HALO = 12
WIDE = ROWS + 2 * HALO

shift_real = 0.5
level_step = 0.4
basis_scale = 16.0
ridge_share = 0.001
bloch_steps = 16.0


VMEM = pl.BlockSpec(memory_space=pltpu.VMEM)
SMEM = pl.BlockSpec(memory_space=pltpu.SMEM)
HBM = pl.BlockSpec(memory_space=pltpu.HBM)
LIMIT = 16 * 1024 * 1024
PAIRS = [(j, k) for j in range(S + 1) for k in range(j, S + 1) if k > 0]
BLOCK = (NZ, LANES)


def vmem(shape):
    return pltpu.VMEM(shape, jnp.float32)


def lane_index(rows):
    return lax.broadcasted_iota(jnp.int32, (rows, LANES), 1)


def roll_lanes(value, shift):
    shift = shift % LANES
    return pltpu.roll(value, shift, 1) if shift else value


def column_order(transposed):
    row = lax.broadcasted_iota(jnp.int32, (LANES, LANES), 0)
    lane = lax.broadcasted_iota(jnp.int32, (LANES, LANES), 1)
    column, place = (lane, row) if transposed else (row, lane)
    wanted = jnp.where(place < 64, 2 * place, 2 * place - (LANES - 1))
    return jnp.where(column == wanted, 1.0, 0.0).astype(jnp.bfloat16)


def reorder(value, order):
    first = value.astype(jnp.bfloat16)
    rest = value - first.astype(jnp.float32)
    second = rest.astype(jnp.bfloat16)
    third = (rest - second.astype(jnp.float32)).astype(jnp.bfloat16)
    parts = [jnp.dot(part, order, preferred_element_type=jnp.float32) for part in (first, second, third)]
    return (parts[0] + parts[1]) + parts[2]


def pack_kernel(rs_hbm, cond_hbm, tile_ref, last_ref, first_ref, strip_ref, rs_ref, cond_ref, sems):
    copies = [
        pltpu.make_async_copy(rs_hbm, rs_ref, sems.at[0]),
        pltpu.make_async_copy(cond_hbm, cond_ref, sems.at[1]),
    ]
    for copy in copies:
        copy.start()
    order = column_order(False)
    eighth = (lane_index(NZ) // 8) % 8

    def pack(source, offset):
        def body(group, _):
            start = (group - offset) * (NZ * ROWS)
            rows = [source[pl.ds(start + x, NZ, stride=ROWS), :] for x in range(ROWS)]
            packed = reorder(jnp.concatenate(rows, axis=0), order)
            rows = [packed[NZ * x : NZ * x + NZ] for x in range(ROWS)]
            for x in range(ROWS):
                tile_ref[group, x] = rows[x]
                if x >= ROWS - HALO:
                    last_ref[group, x - (ROWS - HALO)] = rows[x]
                if x < HALO:
                    first_ref[group, x] = rows[x]
            for four in range(ROWS // 4):
                strip = None
                for j in range(4):
                    moved = roll_lanes(rows[4 * four + j], 64 + 16 * j)
                    if strip is None:
                        strip = moved
                    else:
                        strip = jnp.where((eighth == 2 * j) | (eighth == (7 + 2 * j) % 8), moved, strip)
                strip_ref[group, four] = strip
            return 0

        return body

    copies[0].wait()
    lax.fori_loop(0, 6, pack(rs_ref, 0), 0)
    copies[1].wait()
    lax.fori_loop(6, 9, pack(cond_ref, 6), 0)


def pack_messages(right_side, conductivity):
    rows, edge = (9, ROWS) + BLOCK, (9, HALO) + BLOCK
    return pl.pallas_call(
        pack_kernel,
        out_shape=(vmem(rows), vmem(edge), vmem(edge), vmem((9, ROWS // 4) + BLOCK)),
        in_specs=[HBM, HBM],
        out_specs=(VMEM,) * 4,
        scratch_shapes=[vmem((6 * NZ * ROWS, LANES)), vmem((3 * NZ * ROWS, LANES)), pltpu.SemaphoreType.DMA((2,))],
        compiler_params=pltpu.CompilerParams(vmem_limit_bytes=LIMIT),
        name="pack_messages",
    )(right_side.reshape(6 * NZ * ROWS, LANES), conductivity.reshape(3 * NZ * ROWS, LANES))


def turn(real, imag, cosine, sine):
    return real * cosine - imag * sine, real * sine + imag * cosine


def fill(scal_ref, tile_ref, last_ref, first_ref, sides_ref, above_ref, below_ref, basis_ref, sigma_ref):
    lanes = lane_index(NZ)
    own = lanes < 64
    low_c, low_s, high_c, high_s = (scal_ref[k] for k in range(4))
    cos_y = jnp.where(own, 1.0, jnp.where(lanes < 96, scal_ref[6], scal_ref[4]))
    sin_y = jnp.where(own, 0.0, jnp.where(lanes < 96, scal_ref[7], scal_ref[5]))

    def region(rows_ref, strips_ref, count, base, cosine, sine):
        def body(step, _):
            four, comp = step // 3, step % 3
            for j in range(4):
                x = 4 * four + j

                def pair(group):
                    row = rows_ref[group, x]
                    side = roll_lanes(strips_ref[group, four], -16 * j)
                    return jnp.where(own, row, side), roll_lanes(jnp.where(own, side, row), 64)

                real, imag, sigma = pair(comp), pair(comp + 3), pair(comp + 6)
                for b in range(2):
                    new_real, new_imag = turn(real[b], imag[b], cosine, sine)
                    basis_ref[0, 0, comp, base + x, b] = new_real
                    basis_ref[0, 1, comp, base + x, b] = new_imag
                    sigma_ref[comp, base + x, b] = level_step * sigma[b]
            return 0

        lax.fori_loop(0, 3 * count // 4, body, 0)

    region(last_ref, above_ref, HALO, 0, *turn(cos_y, sin_y, low_c, low_s))
    region(tile_ref, sides_ref, ROWS, HALO, cos_y, sin_y)
    region(first_ref, below_ref, HALO, HALO + ROWS, *turn(cos_y, sin_y, high_c, high_s))


def minus(a, b):
    return a[0] - b[0], a[1] - b[1]


def apply_step(basis_ref, sigma_ref, k, begin, end):
    layer = lax.broadcasted_iota(jnp.int32, BLOCK, 0)
    top, bottom = layer == NZ - 1, layer == 0
    zero = jnp.zeros(BLOCK, jnp.float32)

    def ahead_z(pair):
        return tuple(jnp.where(top, zero, pltpu.roll(v, NZ - 1, 0)) - v for v in pair)

    def back_z(pair):
        return tuple(jnp.where(bottom, zero, pltpu.roll(v, 1, 0)) - v for v in pair)

    def ahead_y(pair):
        return pair[1] - pair[0], roll_lanes(pair[0], -1) - pair[1]

    def back_y(pair):
        return roll_lanes(pair[1], 1) - pair[0], pair[0] - pair[1]

    def load(ri, c, x):
        return basis_ref[k, ri, c, x, 0], basis_ref[k, ri, c, x, 1]

    def curls(ri, x):
        ex, ey, ez = (load(ri, c, x) for c in range(3))
        hy = minus(ahead_z(ex), minus(load(ri, 2, x + 1), ez))
        hz = minus(minus(load(ri, 1, x + 1), ey), ahead_y(ex))
        return ey, ez, hy, hz

    def row(x, carry):
        fresh, outs = [], []
        for ri in range(2):
            ey, ez, hy, hz = curls(ri, x)
            hx = minus(ahead_y(ez), ahead_z(ey))
            old_y, old_z = carry[2 * ri], carry[2 * ri + 1]
            outs.append(
                (
                    minus(back_z(hy), back_y(hz)),
                    minus(minus(old_z, hz), back_z(hx)),
                    minus(back_y(hx), minus(old_y, hy)),
                )
            )
            fresh += [hy, hz]
        for c in range(3):
            real, imag = load(0, c, x), load(1, c, x)
            for b in range(2):
                sigma = sigma_ref[c, x, b]
                basis_ref[k + 1, 0, c, x, b] = (outs[0][c][b] + shift_real * real[b]) - sigma * imag[b]
                basis_ref[k + 1, 1, c, x, b] = (outs[1][c][b] + shift_real * imag[b]) + sigma * real[b]
        return tuple(fresh)

    count = end - begin
    size = next(n for n in (9, 8, 10, 7, 11, 12, 13, 17, 19, 1) if count % n == 0)

    def body(block, carry):
        for spot in range(size):
            carry = row(begin + block * size + spot, carry)
        return carry

    carry = curls(0, begin - 1)[2:] + curls(1, begin - 1)[2:]
    lax.fori_loop(0, count // size, body, carry)


def tree(values):
    while len(values) > 1:
        values = [a + b for a, b in zip(values[::2], values[1::2])] + values[len(values) // 2 * 2 :]
    return values[0]


def gram(basis_ref, sums_ref, gram_ref):
    def body(x, sums):
        reals, imags = [[] for _ in PAIRS], [[] for _ in PAIRS]
        for c in range(3):
            for b in range(2):
                vs = [[basis_ref[k, ri, c, x, b] for ri in range(2)] for k in range(S + 1)]
                for at, (j, k) in enumerate(PAIRS):
                    reals[at].append(vs[j][0] * vs[k][0] + vs[j][1] * vs[k][1])
                    if j != k:
                        imags[at].append(vs[j][0] * vs[k][1] - vs[j][1] * vs[k][0])
        fresh = [tree(terms) for terms in reals + imags if terms]
        return tuple(total + term for total, term in zip(sums, fresh))

    count = len(PAIRS) + sum(j != k for j, k in PAIRS)
    sums = lax.fori_loop(HALO, HALO + ROWS, body, (jnp.zeros(BLOCK, jnp.float32),) * count)
    own = lane_index(1) < 64
    sums_ref[...] = jnp.zeros((LANES, LANES), jnp.float32)
    for at, total in enumerate(sums):
        sums_ref[at : at + 1, :] = jnp.where(own, jnp.sum(total, axis=0, keepdims=True), 0.0)
    gram_ref[...] = lax.dot_general(
        jnp.ones(gram_ref.shape, jnp.float32),
        sums_ref[...],
        (((1,), (1,)), ((), ())),
        precision=lax.Precision.HIGHEST,
        preferred_element_type=jnp.float32,
    )


def cmul(a, b):
    return a[0] * b[0] - a[1] * b[1], a[0] * b[1] + a[1] * b[0]


def csub(a, b):
    return a[0] - b[0], a[1] - b[1]


def conj(a):
    return a[0], -a[1]


def coefficients(gathered_ref):
    row = jnp.broadcast_to(jnp.sum(gathered_ref[...], axis=0, keepdims=True), (8, LANES))

    def pick(at):
        return jnp.broadcast_to(row[:, at : at + 1], (8, LANES))

    entry, at = {}, len(PAIRS)
    for index, (j, k) in enumerate(PAIRS):
        if j == k:
            entry[j, k] = (pick(index), None)
        else:
            entry[j, k] = (pick(index), pick(at))
            at += 1
    unscale = [basis_scale**-k for k in range(2 * S)]
    diag = [entry[k + 1, k + 1][0] * unscale[2 * k] for k in range(S)]
    extra = (ridge_share / S) * ((diag[0] + diag[1]) + (diag[2] + diag[3]))
    diag = [d + extra for d in diag]
    low = {}
    for j in range(S):
        for k in range(j + 1, S):
            real, imag = entry[j + 1, k + 1]
            low[k, j] = (real * unscale[j + k], -imag * unscale[j + k])
    load = [(entry[0, k + 1][0] * unscale[k], -entry[0, k + 1][1] * unscale[k]) for k in range(S)]
    inverse, unit = [], {}
    for k in range(S):
        inverse.append(1.0 / diag[k])
        for i in range(k + 1, S):
            unit[i, k] = (low[i, k][0] * inverse[k], low[i, k][1] * inverse[k])
        for i in range(k + 1, S):
            real, imag = low[i, k]
            diag[i] = diag[i] - (real * real + imag * imag) * inverse[k]
            for j in range(k + 1, i):
                low[i, j] = csub(low[i, j], cmul(unit[i, k], conj(low[j, k])))
            load[i] = csub(load[i], cmul(unit[i, k], load[k]))
    answer = [None] * S
    for k in reversed(range(S)):
        value = (load[k][0] * inverse[k], load[k][1] * inverse[k])
        for j in range(k + 1, S):
            value = csub(value, cmul(conj(unit[j, k]), answer[j]))
        answer[k] = value
    return [(real[0, 0] * unscale[k], imag[0, 0] * unscale[k]) for k, (real, imag) in enumerate(answer)]


def new_residual(basis_ref, coefs, c, x, b):
    real, imag = basis_ref[0, 0, c, x, b], basis_ref[0, 1, c, x, b]
    for k in range(S):
        part = turn(basis_ref[k + 1, 0, c, x, b], basis_ref[k + 1, 1, c, x, b], *coefs[k])
        real, imag = real - part[0], imag - part[1]
    return real, imag


def solution_part(basis_ref, coefs, c, x, b):
    parts = [turn(basis_ref[k, 0, c, x, b], basis_ref[k, 1, c, x, b], *coefs[k]) for k in range(S)]
    return tuple((parts[0][ri] + parts[1][ri]) + (parts[2][ri] + parts[3][ri]) for ri in range(2))


def first_kernel(
    scal_ref, tile_ref, last_ref, first_ref, sides_ref, above_ref, below_ref,
    basis_ref, sigma_ref, gram_ref, sums_ref,
):
    fill(scal_ref, tile_ref, last_ref, first_ref, sides_ref, above_ref, below_ref, basis_ref, sigma_ref)
    for k in range(S):
        apply_step(basis_ref, sigma_ref, k, k + 1, WIDE - k - 1)
    gram(basis_ref, sums_ref, gram_ref)


def next_kernel(sweep, gathered_ref, old_ref, sigma_ref, *refs):
    if sweep == 1:
        basis_ref, part_ref, gram_ref, sums_ref = refs
        old_part = None
    else:
        old_part, basis_ref, part_ref, gram_ref, sums_ref = refs
    coefs = coefficients(gathered_ref)
    begin, end = S * sweep, WIDE - S * sweep

    def residual_row(x, _):
        for c in range(3):
            for b in range(2):
                real, imag = new_residual(old_ref, coefs, c, x, b)
                basis_ref[0, 0, c, x, b] = real
                basis_ref[0, 1, c, x, b] = imag
        return 0

    def tile_row(x, _):
        residual_row(x, 0)
        for c in range(3):
            for b in range(2):
                part = solution_part(old_ref, coefs, c, x, b)
                for ri in range(2):
                    value = part[ri] if old_part is None else part[ri] + old_part[ri, c, x - HALO, b]
                    part_ref[ri, c, x - HALO, b] = value
        return 0

    lax.fori_loop(begin, HALO, residual_row, 0)
    lax.fori_loop(HALO, HALO + ROWS, tile_row, 0)
    lax.fori_loop(HALO + ROWS, end, residual_row, 0)
    for k in range(S):
        apply_step(basis_ref, sigma_ref, k, begin + k + 1, end - k - 1)
    gram(basis_ref, sums_ref, gram_ref)


def last_kernel(gathered_ref, old_ref, old_part, part_ref, residual_ref):
    coefs = coefficients(gathered_ref)
    own = lane_index(NZ) < 64
    order = column_order(True)

    def store(out_ref, group, blocks):
        packed = [jnp.where(own, even, roll_lanes(odd, 64)) for even, odd in blocks]
        rows = reorder(jnp.concatenate(packed, axis=0), order)
        for x in range(ROWS):
            out_ref[pl.ds(group * (NZ * ROWS) + x, NZ, stride=ROWS), :] = rows[NZ * x : NZ * x + NZ]

    def body(c, _):
        residual, part = ([[], []] for _ in range(2))
        for x in range(ROWS):
            rs = [new_residual(old_ref, coefs, c, HALO + x, b) for b in range(2)]
            ps = [solution_part(old_ref, coefs, c, HALO + x, b) for b in range(2)]
            for ri in range(2):
                residual[ri].append((rs[0][ri], rs[1][ri]))
                part[ri].append(tuple(ps[b][ri] + old_part[ri, c, x, b] for b in range(2)))
        for ri in range(2):
            store(residual_ref, 3 * ri + c, residual[ri])
            store(part_ref, 3 * ri + c, part[ri])
        return 0

    lax.fori_loop(0, 3, body, 0)


BASIS = (S + 1, 2, 3, WIDE, 2) + BLOCK
PART = (2, 3, ROWS, 2) + BLOCK


def run_first(peers, *operands):
    return pl.pallas_call(
        first_kernel,
        out_shape=(
            vmem(BASIS), vmem((3, WIDE, 2) + BLOCK), jax.ShapeDtypeStruct((peers, LANES), jnp.float32)
        ),
        in_specs=[SMEM] + [VMEM] * 6,
        out_specs=(VMEM,) * 3,
        scratch_shapes=[vmem((LANES, LANES))],
        compiler_params=pltpu.CompilerParams(vmem_limit_bytes=LIMIT),
        name="first_sweep",
    )(*operands)


def run_next(peers, sweep, *operands):
    return pl.pallas_call(
        functools.partial(next_kernel, sweep),
        out_shape=(vmem(BASIS), vmem(PART), jax.ShapeDtypeStruct((peers, LANES), jnp.float32)),
        in_specs=[VMEM] * len(operands),
        out_specs=(VMEM,) * 3,
        scratch_shapes=[vmem((LANES, LANES))],
        compiler_params=pltpu.CompilerParams(vmem_limit_bytes=LIMIT),
        name="second_sweep" if sweep == 1 else "third_sweep",
    )(*operands)


def run_last(*operands):
    shape = jax.ShapeDtypeStruct((6 * NZ * ROWS, LANES), jnp.float32)
    outs = pl.pallas_call(
        last_kernel,
        out_shape=(shape, shape),
        in_specs=[VMEM] * 3,
        out_specs=(VMEM,) * 2,
        compiler_params=pltpu.CompilerParams(vmem_limit_bytes=LIMIT),
        name="last_update",
    )(*operands)
    return tuple(out.reshape(2, 3, NZ, ROWS, LANES) for out in outs)


def spread(partial):
    return lax.all_to_all(partial, ("gx", "gy"), 0, 0, tiled=True)


def phases(bloch_index):
    theta = 2.0 * math.pi * bloch_index.astype(jnp.float32) / bloch_steps
    rows = []
    for axis, angle in (("gx", theta[0]), ("gy", theta[1])):
        spot, peers = lax.axis_index(axis), lax.axis_size(axis)
        cosine, sine = jnp.cos(angle), jnp.sin(angle)
        rows += [jnp.where(spot == 0, cosine, 1.0), jnp.where(spot == 0, -sine, 0.0)]
        rows += [jnp.where(spot == peers - 1, cosine, 1.0), jnp.where(spot == peers - 1, sine, 0.0)]
    return jnp.stack(rows)


def ring(axis, step):
    peers = lax.axis_size(axis)
    return [(i, (i + step) % peers) for i in range(peers)]


def shards(right_side, conductivity, bloch_index):
    peers = lax.axis_size("gx") * lax.axis_size("gy")
    scal = phases(bloch_index)
    tile, last, first, strips = pack_messages(right_side, conductivity)
    before = lax.ppermute(strips, "gy", ring("gy", 1))
    after = lax.ppermute(strips, "gy", ring("gy", -1))
    above = lax.ppermute(last, "gx", ring("gx", 1))
    below = lax.ppermute(first, "gx", ring("gx", -1))
    from_left = (lax.broadcasted_iota(jnp.int32, strips.shape, 3) // 8) % 2 == 1
    sides = jnp.where(from_left, before, after)
    corners_above = lax.ppermute(sides[:, 1:], "gx", ring("gx", 1))
    corners_below = lax.ppermute(sides[:, :-1], "gx", ring("gx", -1))
    basis, sigma, partial = run_first(peers, scal, tile, above, below, sides, corners_above, corners_below)
    basis, part, partial = run_next(peers, 1, spread(partial), basis, sigma)
    basis, part, partial = run_next(peers, 2, spread(partial), basis, sigma, part)
    return run_last(spread(partial), basis, part)


def solution(mesh):
    in_specs = (P(None, None, None, "gx", "gy"), P(None, None, "gx", "gy"), P())
    out_specs = (P(None, None, None, "gx", "gy"), P(None, None, None, "gx", "gy"))
    return jax.shard_map(shards, mesh=mesh, in_specs=in_specs, out_specs=out_specs, check_vma=False)
```

```python
import functools
import math

import jax
import jax.numpy as jnp
import numpy as np
from jax import lax
from jax.experimental import pallas as pl
from jax.experimental.pallas import tpu as pltpu
from jax.sharding import PartitionSpec as P

S = 4
NZ = 8
ROWS = 16
LANES = 128
HALO = 12
WIDE = ROWS + 2 * HALO

shift_real = 0.5
level_step = 0.4
basis_scale = 16.0
ridge_share = 0.001
bloch_steps = 16.0


VMEM = pl.BlockSpec(memory_space=pltpu.VMEM)
SMEM = pl.BlockSpec(memory_space=pltpu.SMEM)
HBM = pl.BlockSpec(memory_space=pltpu.HBM)
LIMIT = 16 * 1024 * 1024
PAIRS = [(j, k) for j in range(S + 1) for k in range(j, S + 1) if k > 0]
BLOCK = (NZ, LANES)

DEGREE = 2 * S
CENTER = (6.25, 0.75)
BETA = 8.5
SPREAD_MAX = 3.0e4
BIG_PAIRS = [(a, a) for a in range(DEGREE + 1)] + [(a, b) for a in range(DEGREE + 1) for b in range(a + 1, DEGREE + 1)]
BIG_COUNT = len(BIG_PAIRS) + DEGREE * (DEGREE + 1) // 2
ALL_PAIRS = [(0, 0)] + PAIRS


def vmem(shape):
    return pltpu.VMEM(shape, jnp.float32)


def lane_index(rows):
    return lax.broadcasted_iota(jnp.int32, (rows, LANES), 1)


def roll_lanes(value, shift):
    shift = shift % LANES
    return pltpu.roll(value, shift, 1) if shift else value


def column_order(transposed):
    row = lax.broadcasted_iota(jnp.int32, (LANES, LANES), 0)
    lane = lax.broadcasted_iota(jnp.int32, (LANES, LANES), 1)
    column, place = (lane, row) if transposed else (row, lane)
    wanted = jnp.where(place < 64, 2 * place, 2 * place - (LANES - 1))
    return jnp.where(column == wanted, 1.0, 0.0).astype(jnp.bfloat16)


def reorder(value, order):
    first = value.astype(jnp.bfloat16)
    rest = value - first.astype(jnp.float32)
    second = rest.astype(jnp.bfloat16)
    third = (rest - second.astype(jnp.float32)).astype(jnp.bfloat16)
    parts = [jnp.dot(part, order, preferred_element_type=jnp.float32) for part in (first, second, third)]
    return (parts[0] + parts[1]) + parts[2]


def pack_kernel(rs_hbm, cond_hbm, tile_ref, last_ref, first_ref, strip_ref, rs_ref, cond_ref, sems):
    copies = [
        pltpu.make_async_copy(rs_hbm, rs_ref, sems.at[0]),
        pltpu.make_async_copy(cond_hbm, cond_ref, sems.at[1]),
    ]
    for copy in copies:
        copy.start()
    order = column_order(False)
    eighth = (lane_index(NZ) // 8) % 8

    def pack(source, offset):
        def body(group, _):
            start = (group - offset) * (NZ * ROWS)
            rows = [source[pl.ds(start + x, NZ, stride=ROWS), :] for x in range(ROWS)]
            packed = reorder(jnp.concatenate(rows, axis=0), order)
            rows = [packed[NZ * x : NZ * x + NZ] for x in range(ROWS)]
            for x in range(ROWS):
                tile_ref[group, x] = rows[x]
                if x >= ROWS - HALO:
                    last_ref[group, x - (ROWS - HALO)] = rows[x]
                if x < HALO:
                    first_ref[group, x] = rows[x]
            for four in range(ROWS // 4):
                strip = None
                for j in range(4):
                    moved = roll_lanes(rows[4 * four + j], 64 + 16 * j)
                    if strip is None:
                        strip = moved
                    else:
                        strip = jnp.where((eighth == 2 * j) | (eighth == (7 + 2 * j) % 8), moved, strip)
                strip_ref[group, four] = strip
            return 0

        return body

    copies[0].wait()
    lax.fori_loop(0, 6, pack(rs_ref, 0), 0)
    copies[1].wait()
    lax.fori_loop(6, 9, pack(cond_ref, 6), 0)


def pack_messages(right_side, conductivity):
    rows, edge = (9, ROWS) + BLOCK, (9, HALO) + BLOCK
    return pl.pallas_call(
        pack_kernel,
        out_shape=(vmem(rows), vmem(edge), vmem(edge), vmem((9, ROWS // 4) + BLOCK)),
        in_specs=[HBM, HBM],
        out_specs=(VMEM,) * 4,
        scratch_shapes=[vmem((6 * NZ * ROWS, LANES)), vmem((3 * NZ * ROWS, LANES)), pltpu.SemaphoreType.DMA((2,))],
        compiler_params=pltpu.CompilerParams(vmem_limit_bytes=LIMIT),
        name="pack_messages",
    )(right_side.reshape(6 * NZ * ROWS, LANES), conductivity.reshape(3 * NZ * ROWS, LANES))


def turn(real, imag, cosine, sine):
    return real * cosine - imag * sine, real * sine + imag * cosine


def fill(scal_ref, tile_ref, last_ref, first_ref, sides_ref, above_ref, below_ref, basis_ref, sigma_ref):
    lanes = lane_index(NZ)
    own = lanes < 64
    low_c, low_s, high_c, high_s = (scal_ref[k] for k in range(4))
    cos_y = jnp.where(own, 1.0, jnp.where(lanes < 96, scal_ref[6], scal_ref[4]))
    sin_y = jnp.where(own, 0.0, jnp.where(lanes < 96, scal_ref[7], scal_ref[5]))

    def region(rows_ref, strips_ref, count, base, cosine, sine):
        def body(step, _):
            four, comp = step // 3, step % 3
            for j in range(4):
                x = 4 * four + j

                def pair(group):
                    row = rows_ref[group, x]
                    side = roll_lanes(strips_ref[group, four], -16 * j)
                    return jnp.where(own, row, side), roll_lanes(jnp.where(own, side, row), 64)

                real, imag, sigma = pair(comp), pair(comp + 3), pair(comp + 6)
                for b in range(2):
                    new_real, new_imag = turn(real[b], imag[b], cosine, sine)
                    basis_ref[0, 0, comp, base + x, b] = new_real
                    basis_ref[0, 1, comp, base + x, b] = new_imag
                    sigma_ref[comp, base + x, b] = level_step * sigma[b]
            return 0

        lax.fori_loop(0, 3 * count // 4, body, 0)

    region(last_ref, above_ref, HALO, 0, *turn(cos_y, sin_y, low_c, low_s))
    region(tile_ref, sides_ref, ROWS, HALO, cos_y, sin_y)
    region(first_ref, below_ref, HALO, HALO + ROWS, *turn(cos_y, sin_y, high_c, high_s))


def minus(a, b):
    return a[0] - b[0], a[1] - b[1]


def apply_step(basis_ref, sigma_ref, k, begin, end, slots=None):
    before, here, there = (None, k, k + 1) if slots is None else slots
    beta = 0.0 if k == 0 else 2 * BETA if k == 1 else BETA
    layer = lax.broadcasted_iota(jnp.int32, BLOCK, 0)
    top, bottom = layer == NZ - 1, layer == 0
    zero = jnp.zeros(BLOCK, jnp.float32)

    def ahead_z(pair):
        return tuple(jnp.where(top, zero, pltpu.roll(v, NZ - 1, 0)) - v for v in pair)

    def back_z(pair):
        return tuple(jnp.where(bottom, zero, pltpu.roll(v, 1, 0)) - v for v in pair)

    def ahead_y(pair):
        return pair[1] - pair[0], roll_lanes(pair[0], -1) - pair[1]

    def back_y(pair):
        return roll_lanes(pair[1], 1) - pair[0], pair[0] - pair[1]

    def load(ri, c, x):
        return basis_ref[here, ri, c, x, 0], basis_ref[here, ri, c, x, 1]

    def curls(ri, x):
        ex, ey, ez = (load(ri, c, x) for c in range(3))
        hy = minus(ahead_z(ex), minus(load(ri, 2, x + 1), ez))
        hz = minus(minus(load(ri, 1, x + 1), ey), ahead_y(ex))
        return ey, ez, hy, hz

    def row(x, carry):
        fresh, outs = [], []
        for ri in range(2):
            ey, ez, hy, hz = curls(ri, x)
            hx = minus(ahead_y(ez), ahead_z(ey))
            old_y, old_z = carry[2 * ri], carry[2 * ri + 1]
            outs.append(
                (
                    minus(back_z(hy), back_y(hz)),
                    minus(minus(old_z, hz), back_z(hx)),
                    minus(back_y(hx), minus(old_y, hy)),
                )
            )
            fresh += [hy, hz]
        for c in range(3):
            real, imag = load(0, c, x), load(1, c, x)
            for b in range(2):
                sigma = sigma_ref[c, x, b]
                shift = shift_real
                if slots is not None:
                    sigma, shift = sigma - CENTER[1], shift_real - CENTER[0]
                new_real = (outs[0][c][b] + shift * real[b]) - sigma * imag[b]
                new_imag = (outs[1][c][b] + shift * imag[b]) + sigma * real[b]
                if slots is not None and k > 0:
                    new_real = new_real - beta * basis_ref[before, 0, c, x, b]
                    new_imag = new_imag - beta * basis_ref[before, 1, c, x, b]
                basis_ref[there, 0, c, x, b] = new_real
                basis_ref[there, 1, c, x, b] = new_imag
        return tuple(fresh)

    count = end - begin
    size = next(n for n in (9, 8, 10, 7, 11, 12, 13, 17, 19, 1) if count % n == 0)

    def body(block, carry):
        for spot in range(size):
            carry = row(begin + block * size + spot, carry)
        return carry

    carry = curls(0, begin - 1)[2:] + curls(1, begin - 1)[2:]
    lax.fori_loop(0, count // size, body, carry)


def tree(values):
    while len(values) > 1:
        values = [a + b for a, b in zip(values[::2], values[1::2])] + values[len(values) // 2 * 2 :]
    return values[0]


def gram(basis_ref, sums_ref, gram_ref):
    def body(x, sums):
        reals, imags = [[] for _ in PAIRS], [[] for _ in PAIRS]
        for c in range(3):
            for b in range(2):
                vs = [[basis_ref[k, ri, c, x, b] for ri in range(2)] for k in range(S + 1)]
                for at, (j, k) in enumerate(PAIRS):
                    reals[at].append(vs[j][0] * vs[k][0] + vs[j][1] * vs[k][1])
                    if j != k:
                        imags[at].append(vs[j][0] * vs[k][1] - vs[j][1] * vs[k][0])
        fresh = [tree(terms) for terms in reals + imags if terms]
        return tuple(total + term for total, term in zip(sums, fresh))

    count = len(PAIRS) + sum(j != k for j, k in PAIRS)
    sums = lax.fori_loop(HALO, HALO + ROWS, body, (jnp.zeros(BLOCK, jnp.float32),) * count)
    own = lane_index(1) < 64
    sums_ref[...] = jnp.zeros((LANES, LANES), jnp.float32)
    for at, total in enumerate(sums):
        sums_ref[at : at + 1, :] = jnp.where(own, jnp.sum(total, axis=0, keepdims=True), 0.0)
    total_lanes(sums_ref, gram_ref)


def total_lanes(sums_ref, gram_ref):
    gram_ref[...] = lax.dot_general(
        jnp.ones(gram_ref.shape, jnp.float32),
        sums_ref[...],
        (((1,), (1,)), ((), ())),
        precision=lax.Precision.HIGHEST,
        preferred_element_type=jnp.float32,
    )


def cmul(a, b):
    return a[0] * b[0] - a[1] * b[1], a[0] * b[1] + a[1] * b[0]


def csub(a, b):
    return a[0] - b[0], a[1] - b[1]


def conj(a):
    return a[0], -a[1]


def solve(entry):
    unscale = [basis_scale**-k for k in range(2 * S)]
    diag = [entry[k + 1, k + 1][0] * unscale[2 * k] for k in range(S)]
    extra = (ridge_share / S) * ((diag[0] + diag[1]) + (diag[2] + diag[3]))
    diag = [d + extra for d in diag]
    low = {}
    for j in range(S):
        for k in range(j + 1, S):
            real, imag = entry[j + 1, k + 1]
            low[k, j] = (real * unscale[j + k], -imag * unscale[j + k])
    load = [(entry[0, k + 1][0] * unscale[k], -entry[0, k + 1][1] * unscale[k]) for k in range(S)]
    inverse, unit = [], {}
    for k in range(S):
        inverse.append(1.0 / diag[k])
        for i in range(k + 1, S):
            unit[i, k] = (low[i, k][0] * inverse[k], low[i, k][1] * inverse[k])
        for i in range(k + 1, S):
            real, imag = low[i, k]
            diag[i] = diag[i] - (real * real + imag * imag) * inverse[k]
            for j in range(k + 1, i):
                low[i, j] = csub(low[i, j], cmul(unit[i, k], conj(low[j, k])))
            load[i] = csub(load[i], cmul(unit[i, k], load[k]))
    answer = [None] * S
    for k in reversed(range(S)):
        value = (load[k][0] * inverse[k], load[k][1] * inverse[k])
        for j in range(k + 1, S):
            value = csub(value, cmul(conj(unit[j, k]), answer[j]))
        answer[k] = value
    return [(real * unscale[k], imag * unscale[k]) for k, (real, imag) in enumerate(answer)]


def coefficients(gathered_ref):
    row = jnp.broadcast_to(jnp.sum(gathered_ref[...], axis=0, keepdims=True), BLOCK)

    def pick(at):
        return jnp.broadcast_to(row[:, at : at + 1], BLOCK)

    entry, at = {}, len(PAIRS)
    for index, (j, k) in enumerate(PAIRS):
        if j == k:
            entry[j, k] = (pick(index), None)
        else:
            entry[j, k] = (pick(index), pick(at))
            at += 1
    return [(real[0, 0], imag[0, 0]) for real, imag in solve(entry)]


def new_residual(basis_ref, coefs, c, x, b):
    real, imag = basis_ref[0, 0, c, x, b], basis_ref[0, 1, c, x, b]
    for k in range(S):
        part = turn(basis_ref[k + 1, 0, c, x, b], basis_ref[k + 1, 1, c, x, b], *coefs[k])
        real, imag = real - part[0], imag - part[1]
    return real, imag


def solution_part(basis_ref, coefs, c, x, b):
    parts = [turn(basis_ref[k, 0, c, x, b], basis_ref[k, 1, c, x, b], *coefs[k]) for k in range(S)]
    return tuple((parts[0][ri] + parts[1][ri]) + (parts[2][ri] + parts[3][ri]) for ri in range(2))


def first_kernel(
    scal_ref, tile_ref, last_ref, first_ref, sides_ref, above_ref, below_ref,
    basis_ref, sigma_ref, gram_ref, sums_ref,
):
    fill(scal_ref, tile_ref, last_ref, first_ref, sides_ref, above_ref, below_ref, basis_ref, sigma_ref)
    for k in range(S):
        apply_step(basis_ref, sigma_ref, k, k + 1, WIDE - k - 1)
    gram(basis_ref, sums_ref, gram_ref)


def next_kernel(sweep, gathered_ref, old_ref, sigma_ref, *refs):
    if sweep == 1:
        basis_ref, part_ref, gram_ref, sums_ref = refs
        old_part = None
    else:
        old_part, basis_ref, part_ref, gram_ref, sums_ref = refs
    coefs = coefficients(gathered_ref)
    begin, end = S * sweep, WIDE - S * sweep

    def residual_row(x, _):
        for c in range(3):
            for b in range(2):
                real, imag = new_residual(old_ref, coefs, c, x, b)
                basis_ref[0, 0, c, x, b] = real
                basis_ref[0, 1, c, x, b] = imag
        return 0

    def tile_row(x, _):
        residual_row(x, 0)
        for c in range(3):
            for b in range(2):
                part = solution_part(old_ref, coefs, c, x, b)
                for ri in range(2):
                    value = part[ri] if old_part is None else part[ri] + old_part[ri, c, x - HALO, b]
                    part_ref[ri, c, x - HALO, b] = value
        return 0

    lax.fori_loop(begin, HALO, residual_row, 0)
    lax.fori_loop(HALO, HALO + ROWS, tile_row, 0)
    lax.fori_loop(HALO + ROWS, end, residual_row, 0)
    for k in range(S):
        apply_step(basis_ref, sigma_ref, k, begin + k + 1, end - k - 1)
    gram(basis_ref, sums_ref, gram_ref)


def last_kernel(gathered_ref, old_ref, old_part, part_ref, residual_ref):
    coefs = coefficients(gathered_ref)
    own = lane_index(NZ) < 64
    order = column_order(True)

    def store(out_ref, group, blocks):
        packed = [jnp.where(own, even, roll_lanes(odd, 64)) for even, odd in blocks]
        rows = reorder(jnp.concatenate(packed, axis=0), order)
        for x in range(ROWS):
            out_ref[pl.ds(group * (NZ * ROWS) + x, NZ, stride=ROWS), :] = rows[NZ * x : NZ * x + NZ]

    def body(c, _):
        residual, part = ([[], []] for _ in range(2))
        for x in range(ROWS):
            rs = [new_residual(old_ref, coefs, c, HALO + x, b) for b in range(2)]
            ps = [solution_part(old_ref, coefs, c, HALO + x, b) for b in range(2)]
            for ri in range(2):
                residual[ri].append((rs[0][ri], rs[1][ri]))
                part[ri].append(tuple(ps[b][ri] + old_part[ri, c, x, b] for b in range(2)))
        for ri in range(2):
            store(residual_ref, 3 * ri + c, residual[ri])
            store(part_ref, 3 * ri + c, part[ri])
        return 0

    lax.fori_loop(0, 3, body, 0)


def two_sum(a, b):
    total = a + b
    other = total - a
    return total, (a - (total - other)) + (b - other)


def quick_sum(a, b):
    total = a + b
    return total, b - (total - a)


def pair_sum(a, b):
    total, error = two_sum(a[0], b[0])
    return quick_sum(total, error + (a[1] + b[1]))


def halves(a):
    scaled = a * 4097.0
    high = scaled - (scaled - a)
    return high, a - high


def two_product(a, b):
    product = a * b
    (ah, al), (bh, bl) = halves(a), halves(b)
    return product, ((ah * bh - product) + ah * bl + al * bh) + al * bl


def pair_product(a, b):
    product, error = two_product(a[0], b[0])
    return quick_sum(product, error + (a[0] * b[1] + a[1] * b[0]))


def negative(a):
    return -a[0], -a[1]


def choose(mask, a, b):
    return jnp.where(mask, a[0], b[0]), jnp.where(mask, a[1], b[1])


def all_lanes(value):
    for step in (64, 32, 16, 8, 4, 2, 1):
        value = pair_sum(value, tuple(roll_lanes(part, step) for part in value))
    return value


def all_devices(gathered_ref):
    rows = gathered_ref.shape[0] // 2
    value = two_sum(gathered_ref[:rows, :], gathered_ref[rows:, :])
    while rows > 8:
        rows = rows // 2
        value = pair_sum(tuple(v[:rows] for v in value), tuple(v[rows:] for v in value))
    step = rows // 2
    while step:
        value = pair_sum(value, tuple(pltpu.roll(v, step, 0) for v in value))
        step = step // 2
    return tuple(jnp.broadcast_to(v[:1], BLOCK) for v in value)


def constants():
    size = DEGREE + 1
    step = np.zeros((size + 1, size), np.complex128)
    for k in range(size):
        step[k, k] = complex(*CENTER)
        step[k + 1, k] = 1.0
        if k:
            step[k - 1, k] = BETA * (2 if k == 1 else 1)
    power = [np.eye(size)[0].astype(np.complex128)]
    for _ in range(S):
        power.append(step[:size] @ power[-1])
    lanes = [(a, b, 0) for a, b in BIG_PAIRS] + [(a, b, 1) for a, b in BIG_PAIRS if a != b]
    table = np.zeros((32, LANES), np.float64)
    pick_a, pick_b = np.zeros((LANES, LANES)), np.zeros((LANES, LANES))
    for lane, (a, b, imag) in enumerate(lanes):
        pick_a[a, lane] = pick_b[b, lane] = 1
        for row, (j, k) in enumerate(ALL_PAIRS):
            first = np.conj(power[j][a]) * power[k][b]
            second = np.conj(power[j][b]) * power[k][a]
            total = first if a == b else 1j * (first - second) if imag else first + second
            table[row, lane], table[16 + row, lane] = total.real, total.imag
    high = table.astype(np.float32)
    low = (table - high).astype(np.float32)
    rows = np.zeros((16, LANES), np.float32)
    for k in range(S + 1):
        rows[k, :size], rows[8 + k, :size] = power[k].real, power[k].imag
    picks = np.stack([pick_a, pick_b]).astype(jnp.bfloat16)
    select = np.zeros((2, 32, 32))
    for row, pair in enumerate(ALL_PAIRS):
        for side in range(2):
            select[side, row, pair[side]] = select[side, 16 + row, 16 + pair[side]] = 1
    return np.concatenate([high, low, rows]), picks, select.astype(jnp.bfloat16)


def pick_rows(select, value):
    first = value.astype(jnp.bfloat16)
    rest = value - first.astype(jnp.float32)
    second = rest.astype(jnp.bfloat16)
    third = (rest - second.astype(jnp.float32)).astype(jnp.bfloat16)
    parts = [jnp.dot(select, part, preferred_element_type=jnp.float32) for part in (first, second, third)]
    return (parts[0] + parts[1]) + parts[2]


def entries(rows):
    return {pair: (rows[p : p + 1], rows[16 + p : 17 + p]) for p, pair in enumerate(ALL_PAIRS)}


def both_iterations(gathered_ref, table_ref, picks_ref, select_ref):
    sums = all_devices(gathered_ref)
    lane = lane_index(1)
    four = tuple(jnp.concatenate([v] * 4, axis=0) for v in sums)
    table = table_ref[0:32, :], table_ref[32:64, :]
    second = entries(all_lanes(pair_product(table, four))[0])
    y = solve(second)
    power = [(table_ref[64 + k : 65 + k, :], table_ref[72 + k : 73 + k, :]) for k in range(S + 1)]
    residual = power[0]
    for k in range(S):
        residual = csub(residual, cmul(y[k], power[k + 1]))
    down = jnp.where(lane == 0, 2 * BETA, jnp.where(lane < DEGREE, BETA, 0.0))
    up = jnp.where((lane > 0) & (lane <= DEGREE), 1.0, 0.0)
    chain = [residual]
    for _ in range(S):
        p = chain[-1]
        side = [down * roll_lanes(v, -1) + up * roll_lanes(v, 1) for v in p]
        turned = cmul(CENTER, p)
        chain.append((turned[0] + side[0], turned[1] + side[1]))
    gap = jnp.zeros((16 - len(chain), LANES), jnp.float32)
    stack = jnp.concatenate([v[0] for v in chain] + [gap] + [v[1] for v in chain] + [gap], axis=0)
    at_a, at_b = reorder(stack, picks_ref[0]), reorder(stack, picks_ref[1])
    aj, ak = pick_rows(select_ref[0], at_a), pick_rows(select_ref[1], at_a)
    bj, bk = pick_rows(select_ref[0], at_b), pick_rows(select_ref[1], at_b)

    def product(left, right):
        (lr, li), (rr, ri) = (left[:16], left[16:]), (right[:16], right[16:])
        real = pair_sum(two_product(lr, rr), two_product(li, ri))
        return real, pair_sum(two_product(lr, ri), negative(two_product(li, rr)))

    lanes16 = lane_index(16)
    whole = len(BIG_PAIRS)
    sign = jnp.where(lanes16 <= DEGREE, 0.0, jnp.where(lanes16 < whole, 1.0, -1.0))
    first, other = product(aj, bk), product(bj, ak)
    real, imag = (pair_sum(f, (sign * o[0], sign * o[1])) for f, o in zip(first, other))
    mixed = lanes16 >= whole
    parts = choose(mixed, negative(imag), real), choose(mixed, real, imag)
    rows = tuple(jnp.concatenate([parts[0][n], parts[1][n]], axis=0) for n in range(2))
    third = entries(all_lanes(pair_product(rows, four))[0])
    z = solve(third)

    norms = jnp.sqrt(jnp.where(lane <= DEGREE, sums[0][:1], 0.0))
    sizes = [jnp.abs(v[0]) + jnp.abs(v[1]) for v in chain + power]
    sizes = jnp.concatenate([size * norms for size in sizes], axis=0)
    for step in (64, 32, 16, 8, 4, 2, 1):
        sizes = sizes + roll_lanes(sizes, step)
    spread = None
    for at, source in ((0, third), (S + 1, second)):
        for k in range(S + 1):
            size = sizes[at + k : at + k + 1]
            ratio = size * size / source[k, k][0]
            spread = ratio if spread is None else jnp.where(ratio < spread, spread, ratio)
    part = None
    for k in range(S):
        term = cmul(y[k], power[k])
        other = cmul(z[k], chain[k])
        term = (term[0] + other[0], term[1] + other[1])
        part = term if part is None else (part[0] + term[0], part[1] + term[1])
        residual = csub(residual, cmul(z[k], chain[k + 1]))
    return part, residual, spread


def packed(even, odd):
    return jnp.where(lane_index(NZ) < 64, even, roll_lanes(odd, 64))


def wide_kernel(gathered_ref, old_ref, sigma_ref, tile_ref, part_ref, gram_ref, basis_ref, acc_ref, sums_ref):
    coefs = coefficients(gathered_ref)
    begin, end = S, WIDE - S

    def residual_row(x, _):
        for c in range(3):
            for b in range(2):
                real, imag = new_residual(old_ref, coefs, c, x, b)
                basis_ref[0, 0, c, x, b] = real
                basis_ref[0, 1, c, x, b] = imag
        return 0

    def tile_row(x, _):
        residual_row(x, 0)
        for c in range(3):
            even, odd = (solution_part(old_ref, coefs, c, x, b) for b in range(2))
            for ri in range(2):
                part_ref[ri, c, x - HALO] = packed(even[ri], odd[ri])
        return 0

    lax.fori_loop(begin, HALO, residual_row, 0)
    lax.fori_loop(HALO, HALO + ROWS, tile_row, 0)
    lax.fori_loop(HALO + ROWS, end, residual_row, 0)
    for k in range(DEGREE):
        apply_step(basis_ref, sigma_ref, k, begin + k + 1, end - k - 1, (k - 1, k, k + 1))
    acc_ref[...] = jnp.zeros(acc_ref.shape, jnp.float32)

    def gram_row(x, _):
        for c in range(3):
            vs = []
            for k in range(DEGREE + 1):
                vs.append([packed(basis_ref[k, ri, c, x, 0], basis_ref[k, ri, c, x, 1]) for ri in range(2)])
                for ri in range(2):
                    tile_ref[k, ri, c, x - HALO] = vs[k][ri]
            at = len(BIG_PAIRS)
            for index, (j, k) in enumerate(BIG_PAIRS):
                acc_ref[index] += vs[j][0] * vs[k][0] + vs[j][1] * vs[k][1]
                if j != k:
                    acc_ref[at] += vs[j][0] * vs[k][1] - vs[j][1] * vs[k][0]
                    at += 1
        return 0

    lax.fori_loop(HALO, HALO + ROWS, gram_row, 0)
    sums_ref[...] = jnp.zeros((LANES, LANES), jnp.float32)
    for at in range(BIG_COUNT):
        sums_ref[at : at + 1, :] = jnp.sum(acc_ref[at], axis=0, keepdims=True)
    total_lanes(sums_ref, gram_ref)


def end_kernel(
    gathered_ref, table_ref, picks_ref, select_ref, tile_ref, old_part, part_ref, residual_ref, spread_ref, coef_ref
):
    part, residual, spread = both_iterations(gathered_ref, table_ref, picks_ref, select_ref)
    spread_ref[...] = jnp.broadcast_to(spread, BLOCK)
    for a in range(DEGREE + 1):
        for n, value in enumerate(part + residual):
            coef_ref[4 * a + n] = jnp.broadcast_to(value[:, a : a + 1], BLOCK)
    order = column_order(True)

    def body(c, _):
        sums = [[] for _ in range(4)]
        for x in range(ROWS):
            totals = [old_part[0, c, x], old_part[1, c, x], None, None]
            for a in range(DEGREE + 1):
                real, imag = tile_ref[a, 0, c, x], tile_ref[a, 1, c, x]
                for out in range(2):
                    if out == 0 and a == DEGREE:
                        continue
                    term = turn(real, imag, coef_ref[4 * a + 2 * out], coef_ref[4 * a + 2 * out + 1])
                    for ri in range(2):
                        old = totals[2 * out + ri]
                        totals[2 * out + ri] = term[ri] if old is None else old + term[ri]
            for n in range(4):
                sums[n].append(totals[n])
        for n in range(4):
            rows = reorder(jnp.concatenate(sums[n], axis=0), order)
            out_ref = residual_ref if n >= 2 else part_ref
            group = 3 * (n % 2) + c
            for x in range(ROWS):
                out_ref[pl.ds(group * (NZ * ROWS) + x, NZ, stride=ROWS), :] = rows[NZ * x : NZ * x + NZ]
        return 0

    lax.fori_loop(0, 3, body, 0)


BASIS = (S + 1, 2, 3, WIDE, 2) + BLOCK
PART = (2, 3, ROWS, 2) + BLOCK


def run_first(peers, *operands):
    return pl.pallas_call(
        first_kernel,
        out_shape=(
            vmem(BASIS), vmem((3, WIDE, 2) + BLOCK), jax.ShapeDtypeStruct((peers, LANES), jnp.float32)
        ),
        in_specs=[SMEM] + [VMEM] * 6,
        out_specs=(VMEM,) * 3,
        scratch_shapes=[vmem((LANES, LANES))],
        compiler_params=pltpu.CompilerParams(vmem_limit_bytes=LIMIT),
        name="first_sweep",
    )(*operands)


def run_next(peers, sweep, *operands):
    return pl.pallas_call(
        functools.partial(next_kernel, sweep),
        out_shape=(vmem(BASIS), vmem(PART), jax.ShapeDtypeStruct((peers, LANES), jnp.float32)),
        in_specs=[VMEM] * len(operands),
        out_specs=(VMEM,) * 3,
        scratch_shapes=[vmem((LANES, LANES))],
        compiler_params=pltpu.CompilerParams(vmem_limit_bytes=LIMIT),
        name="second_sweep" if sweep == 1 else "third_sweep",
    )(*operands)


def run_wide(peers, *operands):
    return pl.pallas_call(
        wide_kernel,
        out_shape=(
            vmem((DEGREE + 1, 2, 3, ROWS) + BLOCK),
            vmem((2, 3, ROWS) + BLOCK),
            jax.ShapeDtypeStruct((peers, LANES), jnp.float32),
        ),
        in_specs=[VMEM] * 3,
        out_specs=(VMEM,) * 3,
        scratch_shapes=[
            vmem((DEGREE + 1, 2, 3, WIDE, 2) + BLOCK), vmem((BIG_COUNT,) + BLOCK), vmem((LANES, LANES))
        ],
        compiler_params=pltpu.CompilerParams(vmem_limit_bytes=24 * 1024 * 1024),
        name="second_third_basis",
    )(*operands)


def run_end(*operands):
    shape = jax.ShapeDtypeStruct((6 * NZ * ROWS, LANES), jnp.float32)
    tables = [jnp.asarray(table) for table in constants()]
    part, residual, spread = pl.pallas_call(
        end_kernel,
        out_shape=(shape, shape, jax.ShapeDtypeStruct(BLOCK, jnp.float32)),
        in_specs=[VMEM] * 6,
        out_specs=(VMEM,) * 3,
        scratch_shapes=[vmem((4 * (DEGREE + 1),) + BLOCK)],
        compiler_params=pltpu.CompilerParams(vmem_limit_bytes=LIMIT),
        name="second_third_update",
    )(operands[0], *tables, *operands[1:])
    return tuple(out.reshape(2, 3, NZ, ROWS, LANES) for out in (part, residual)) + (spread[0, 0],)


def run_last(*operands):
    shape = jax.ShapeDtypeStruct((6 * NZ * ROWS, LANES), jnp.float32)
    outs = pl.pallas_call(
        last_kernel,
        out_shape=(shape, shape),
        in_specs=[VMEM] * 3,
        out_specs=(VMEM,) * 2,
        compiler_params=pltpu.CompilerParams(vmem_limit_bytes=LIMIT),
        name="last_update",
    )(*operands)
    return tuple(out.reshape(2, 3, NZ, ROWS, LANES) for out in outs)


def spread(partial):
    return lax.all_to_all(partial, ("gx", "gy"), 0, 0, tiled=True)


def phases(bloch_index):
    theta = 2.0 * math.pi * bloch_index.astype(jnp.float32) / bloch_steps
    rows = []
    for axis, angle in (("gx", theta[0]), ("gy", theta[1])):
        spot, peers = lax.axis_index(axis), lax.axis_size(axis)
        cosine, sine = jnp.cos(angle), jnp.sin(angle)
        rows += [jnp.where(spot == 0, cosine, 1.0), jnp.where(spot == 0, -sine, 0.0)]
        rows += [jnp.where(spot == peers - 1, cosine, 1.0), jnp.where(spot == peers - 1, sine, 0.0)]
    return jnp.stack(rows)


def ring(axis, step):
    peers = lax.axis_size(axis)
    return [(i, (i + step) % peers) for i in range(peers)]


def first_sweep(right_side, conductivity, bloch_index):
    peers = lax.axis_size("gx") * lax.axis_size("gy")
    scal = phases(bloch_index)
    tile, last, first, strips = pack_messages(right_side, conductivity)
    before = lax.ppermute(strips, "gy", ring("gy", 1))
    after = lax.ppermute(strips, "gy", ring("gy", -1))
    above = lax.ppermute(last, "gx", ring("gx", 1))
    below = lax.ppermute(first, "gx", ring("gx", -1))
    from_left = (lax.broadcasted_iota(jnp.int32, strips.shape, 3) // 8) % 2 == 1
    sides = jnp.where(from_left, before, after)
    corners_above = lax.ppermute(sides[:, 1:], "gx", ring("gx", 1))
    corners_below = lax.ppermute(sides[:, :-1], "gx", ring("gx", -1))
    basis, sigma, partial = run_first(peers, scal, tile, above, below, sides, corners_above, corners_below)
    return peers, basis, sigma, spread(partial)


def three_reductions(*operands):
    peers, basis, sigma, gathered = first_sweep(*operands)
    basis, part, partial = run_next(peers, 1, gathered, basis, sigma)
    basis, part, partial = run_next(peers, 2, spread(partial), basis, sigma, part)
    return run_last(spread(partial), basis, part)


def two_reductions(*operands):
    peers, basis, sigma, gathered = first_sweep(*operands)
    tile, part, partial = run_wide(peers, gathered, basis, sigma)
    return run_end(spread(partial), tile, part)


def shards(*operands):
    part, residual, cancelled = two_reductions(*operands)
    state = (jnp.logical_not(cancelled < SPREAD_MAX), part, residual)

    def again(_):
        return (jnp.array(False),) + three_reductions(*operands)

    return lax.while_loop(lambda state: state[0], again, state)[1:]


def solution(mesh):
    in_specs = (P(None, None, None, "gx", "gy"), P(None, None, "gx", "gy"), P())
    out_specs = (P(None, None, None, "gx", "gy"), P(None, None, None, "gx", "gy"))
    return jax.shard_map(shards, mesh=mesh, in_specs=in_specs, out_specs=out_specs, check_vma=False)
```

```python
import functools
import math

import jax
import jax.numpy as jnp
import numpy as np
from jax import lax
from jax.experimental import pallas as pl
from jax.experimental.pallas import tpu as pltpu
from jax.sharding import PartitionSpec as P

S = 4
NZ = 8
ROWS = 16
LANES = 128
HALO = 12
WIDE = ROWS + 2 * HALO

shift_real = 0.5
level_step = 0.4
basis_scale = 16.0
ridge_share = 0.001
bloch_steps = 16.0


VMEM = pl.BlockSpec(memory_space=pltpu.VMEM)
SMEM = pl.BlockSpec(memory_space=pltpu.SMEM)
HBM = pl.BlockSpec(memory_space=pltpu.HBM)
LIMIT = 16 * 1024 * 1024
PAIRS = [(j, k) for j in range(S + 1) for k in range(j, S + 1) if k > 0]
BLOCK = (NZ, LANES)

DEGREE = 2 * S
CENTER = (6.25, 0.75)
BETA = 8.5
SPREAD_MAX = 3.0e4
BIG_PAIRS = [(a, a) for a in range(DEGREE + 1)] + [(a, b) for a in range(DEGREE + 1) for b in range(a + 1, DEGREE + 1)]
BIG_COUNT = len(BIG_PAIRS) + DEGREE * (DEGREE + 1) // 2
ALL_PAIRS = [(0, 0)] + PAIRS


def vmem(shape):
    return pltpu.VMEM(shape, jnp.float32)


def lane_index(rows):
    return lax.broadcasted_iota(jnp.int32, (rows, LANES), 1)


def roll_lanes(value, shift):
    shift = shift % LANES
    return pltpu.roll(value, shift, 1) if shift else value


def column_order(transposed):
    row = lax.broadcasted_iota(jnp.int32, (LANES, LANES), 0)
    lane = lax.broadcasted_iota(jnp.int32, (LANES, LANES), 1)
    column, place = (lane, row) if transposed else (row, lane)
    wanted = jnp.where(place < 64, 2 * place, 2 * place - (LANES - 1))
    return jnp.where(column == wanted, 1.0, 0.0).astype(jnp.bfloat16)


def reorder(value, order):
    first = value.astype(jnp.bfloat16)
    rest = value - first.astype(jnp.float32)
    second = rest.astype(jnp.bfloat16)
    third = (rest - second.astype(jnp.float32)).astype(jnp.bfloat16)
    parts = [jnp.dot(part, order, preferred_element_type=jnp.float32) for part in (first, second, third)]
    return (parts[0] + parts[1]) + parts[2]


def pack_kernel(rs_hbm, cond_hbm, tile_ref, last_ref, first_ref, strip_ref, rs_ref, cond_ref, sems):
    copies = [
        pltpu.make_async_copy(rs_hbm, rs_ref, sems.at[0]),
        pltpu.make_async_copy(cond_hbm, cond_ref, sems.at[1]),
    ]
    for copy in copies:
        copy.start()
    order = column_order(False)
    eighth = (lane_index(NZ) // 8) % 8

    def pack(source, offset):
        def body(group):
            start = (group - offset) * (NZ * ROWS)
            rows = [source[pl.ds(start + x, NZ, stride=ROWS), :] for x in range(ROWS)]
            mixed = reorder(jnp.concatenate(rows, axis=0), order)
            rows = [mixed[NZ * x : NZ * x + NZ] for x in range(ROWS)]
            for x in range(ROWS):
                tile_ref[group, x] = rows[x]
                if x >= ROWS - HALO:
                    last_ref[group, x - (ROWS - HALO)] = rows[x]
                if x < HALO:
                    first_ref[group, x] = rows[x]
            for four in range(ROWS // 4):
                strip = None
                for j in range(4):
                    moved = roll_lanes(rows[4 * four + j], 64 + 16 * j)
                    if strip is None:
                        strip = moved
                    else:
                        strip = jnp.where((eighth == 2 * j) | (eighth == (7 + 2 * j) % 8), moved, strip)
                strip_ref[group, four] = strip

        return body

    copies[0].wait()
    each(0, 6, 3, pack(rs_ref, 0))
    copies[1].wait()
    each(6, 9, 3, pack(cond_ref, 6))


def pack_messages(right_side, conductivity):
    rows, edge = (9, ROWS) + BLOCK, (9, HALO) + BLOCK
    return pl.pallas_call(
        pack_kernel,
        out_shape=(vmem(rows), vmem(edge), vmem(edge), vmem((9, ROWS // 4) + BLOCK)),
        in_specs=[HBM, HBM],
        out_specs=(VMEM,) * 4,
        scratch_shapes=[vmem((6 * NZ * ROWS, LANES)), vmem((3 * NZ * ROWS, LANES)), pltpu.SemaphoreType.DMA((2,))],
        compiler_params=pltpu.CompilerParams(vmem_limit_bytes=LIMIT),
        name="pack_messages",
    )(right_side.reshape(6 * NZ * ROWS, LANES), conductivity.reshape(3 * NZ * ROWS, LANES))


def each(begin, end, size, body):
    def block(step, _):
        for spot in range(size):
            body(begin + step * size + spot)
        return 0

    lax.fori_loop(0, (end - begin) // size, block, 0)


def turn(real, imag, cosine, sine):
    return real * cosine - imag * sine, real * sine + imag * cosine


def fill_region(scal_ref, rows_ref, strips_ref, count, base, turned, basis_ref, sigma_ref):
    lanes = lane_index(NZ)
    own = lanes < 64
    cosine = jnp.where(own, 1.0, jnp.where(lanes < 96, scal_ref[6], scal_ref[4]))
    sine = jnp.where(own, 0.0, jnp.where(lanes < 96, scal_ref[7], scal_ref[5]))
    if turned is not None:
        cosine, sine = turn(cosine, sine, scal_ref[turned], scal_ref[turned + 1])

    def body(four):
        for comp in range(3):
            for j in range(4):
                x = 4 * four + j

                def pair(group):
                    row = rows_ref[group, x]
                    side = roll_lanes(strips_ref[group, four], -16 * j)
                    return jnp.where(own, row, side), roll_lanes(jnp.where(own, side, row), 64)

                real, imag, sigma = pair(comp), pair(comp + 3), pair(comp + 6)
                for b in range(2):
                    new_real, new_imag = turn(real[b], imag[b], cosine, sine)
                    basis_ref[0, 0, comp, base + x, b] = new_real
                    basis_ref[0, 1, comp, base + x, b] = new_imag
                    sigma_ref[comp, base + x, b] = level_step * sigma[b]

    each(0, count // 4, 1, body)


def minus(a, b):
    return a[0] - b[0], a[1] - b[1]


def apply_step(basis_ref, sigma_ref, k, starts, count, slots=None):
    before, here, there = (None, k, k + 1) if slots is None else slots
    beta = 0.0 if k == 0 else 2 * BETA if k == 1 else BETA
    layer = lax.broadcasted_iota(jnp.int32, BLOCK, 0)
    top, bottom = layer == NZ - 1, layer == 0
    zero = jnp.zeros(BLOCK, jnp.float32)

    def ahead_z(pair):
        return tuple(jnp.where(top, zero, pltpu.roll(v, NZ - 1, 0)) - v for v in pair)

    def back_z(pair):
        return tuple(jnp.where(bottom, zero, pltpu.roll(v, 1, 0)) - v for v in pair)

    def ahead_y(pair):
        return pair[1] - pair[0], roll_lanes(pair[0], -1) - pair[1]

    def back_y(pair):
        return roll_lanes(pair[1], 1) - pair[0], pair[0] - pair[1]

    def load(ri, c, x):
        return basis_ref[here, ri, c, x, 0], basis_ref[here, ri, c, x, 1]

    def curls(ri, x):
        ex, ey, ez = (load(ri, c, x) for c in range(3))
        hy = minus(ahead_z(ex), minus(load(ri, 2, x + 1), ez))
        hz = minus(minus(load(ri, 1, x + 1), ey), ahead_y(ex))
        return ey, ez, hy, hz

    def row(x, carry):
        fresh, outs = [], []
        for ri in range(2):
            ey, ez, hy, hz = curls(ri, x)
            hx = minus(ahead_y(ez), ahead_z(ey))
            old_y, old_z = carry[2 * ri], carry[2 * ri + 1]
            outs.append(
                (
                    minus(back_z(hy), back_y(hz)),
                    minus(minus(old_z, hz), back_z(hx)),
                    minus(back_y(hx), minus(old_y, hy)),
                )
            )
            fresh += [hy, hz]
        for c in range(3):
            real, imag = load(0, c, x), load(1, c, x)
            for b in range(2):
                sigma = sigma_ref[c, x, b]
                shift = shift_real
                if slots is not None:
                    sigma, shift = sigma - CENTER[1], shift_real - CENTER[0]
                new_real = (outs[0][c][b] + shift * real[b]) - sigma * imag[b]
                new_imag = (outs[1][c][b] + shift * imag[b]) + sigma * real[b]
                if slots is not None and k > 0:
                    new_real = new_real - beta * basis_ref[before, 0, c, x, b]
                    new_imag = new_imag - beta * basis_ref[before, 1, c, x, b]
                basis_ref[there, 0, c, x, b] = new_real
                basis_ref[there, 1, c, x, b] = new_imag
        return tuple(fresh)

    size = next(n for n in (9, 8, 10, 7, 11, 12, 13, 17, 19, 1) if count % n == 0) if len(starts) == 1 else 6

    def body(block, carry):
        carry = list(carry)
        for spot in range(size):
            for n, start in enumerate(starts):
                carry[4 * n : 4 * n + 4] = row(start + block * size + spot, carry[4 * n : 4 * n + 4])
        return tuple(carry)

    carry = ()
    for start in starts:
        carry += curls(0, start - 1)[2:] + curls(1, start - 1)[2:]
    lax.fori_loop(0, count // size, body, carry)


def tree(values):
    while len(values) > 1:
        values = [a + b for a, b in zip(values[::2], values[1::2])] + values[len(values) // 2 * 2 :]
    return values[0]


def gram(basis_ref, sums_ref, gram_ref):
    def body(step, sums):
        reals, imags = [[] for _ in PAIRS], [[] for _ in PAIRS]
        for c in range(3):
            for n in range(4):
                x, b = HALO + 2 * step + n // 2, n % 2
                vs = [[basis_ref[k, ri, c, x, b] for ri in range(2)] for k in range(S + 1)]
                for at, (j, k) in enumerate(PAIRS):
                    reals[at].append(vs[j][0] * vs[k][0] + vs[j][1] * vs[k][1])
                    if j != k:
                        imags[at].append(vs[j][0] * vs[k][1] - vs[j][1] * vs[k][0])
        fresh = [tree(terms) for terms in reals + imags if terms]
        return tuple(total + term for total, term in zip(sums, fresh))

    count = len(PAIRS) + sum(j != k for j, k in PAIRS)
    sums = lax.fori_loop(0, ROWS // 2, body, (jnp.zeros(BLOCK, jnp.float32),) * count)
    own = lane_index(1) < 64
    sums_ref[...] = jnp.zeros((LANES, LANES), jnp.float32)
    for at, total in enumerate(sums):
        sums_ref[at : at + 1, :] = jnp.where(own, jnp.sum(total, axis=0, keepdims=True), 0.0)
    total_lanes(sums_ref, gram_ref)


def total_lanes(sums_ref, gram_ref):
    gram_ref[...] = lax.dot_general(
        jnp.ones(gram_ref.shape, jnp.float32),
        sums_ref[...],
        (((1,), (1,)), ((), ())),
        precision=lax.Precision.HIGHEST,
        preferred_element_type=jnp.float32,
    )


def cmul(a, b):
    return a[0] * b[0] - a[1] * b[1], a[0] * b[1] + a[1] * b[0]


def csub(a, b):
    return a[0] - b[0], a[1] - b[1]


def conj(a):
    return a[0], -a[1]


def solve(entry):
    unscale = [basis_scale**-k for k in range(2 * S)]
    diag = [entry[k + 1, k + 1][0] * unscale[2 * k] for k in range(S)]
    extra = (ridge_share / S) * ((diag[0] + diag[1]) + (diag[2] + diag[3]))
    diag = [d + extra for d in diag]
    low = {}
    for j in range(S):
        for k in range(j + 1, S):
            real, imag = entry[j + 1, k + 1]
            low[k, j] = (real * unscale[j + k], -imag * unscale[j + k])
    load = [(entry[0, k + 1][0] * unscale[k], -entry[0, k + 1][1] * unscale[k]) for k in range(S)]
    inverse, unit = [], {}
    for k in range(S):
        inverse.append(1.0 / diag[k])
        for i in range(k + 1, S):
            unit[i, k] = (low[i, k][0] * inverse[k], low[i, k][1] * inverse[k])
        for i in range(k + 1, S):
            real, imag = low[i, k]
            diag[i] = diag[i] - (real * real + imag * imag) * inverse[k]
            for j in range(k + 1, i):
                low[i, j] = csub(low[i, j], cmul(unit[i, k], conj(low[j, k])))
            load[i] = csub(load[i], cmul(unit[i, k], load[k]))
    answer = [None] * S
    for k in reversed(range(S)):
        value = (load[k][0] * inverse[k], load[k][1] * inverse[k])
        for j in range(k + 1, S):
            value = csub(value, cmul(conj(unit[j, k]), answer[j]))
        answer[k] = value
    return [(real * unscale[k], imag * unscale[k]) for k, (real, imag) in enumerate(answer)]


def coefficients(gathered_ref):
    row = jnp.broadcast_to(jnp.sum(gathered_ref[...], axis=0, keepdims=True), BLOCK)

    def pick(at):
        return jnp.broadcast_to(row[:, at : at + 1], BLOCK)

    entry, at = {}, len(PAIRS)
    for index, (j, k) in enumerate(PAIRS):
        if j == k:
            entry[j, k] = (pick(index), None)
        else:
            entry[j, k] = (pick(index), pick(at))
            at += 1
    return [(real[0, 0], imag[0, 0]) for real, imag in solve(entry)]


def new_residual(basis_ref, coefs, c, x, b):
    real, imag = basis_ref[0, 0, c, x, b], basis_ref[0, 1, c, x, b]
    for k in range(S):
        part = turn(basis_ref[k + 1, 0, c, x, b], basis_ref[k + 1, 1, c, x, b], *coefs[k])
        real, imag = real - part[0], imag - part[1]
    return real, imag


def solution_part(basis_ref, coefs, c, x, b):
    parts = [turn(basis_ref[k, 0, c, x, b], basis_ref[k, 1, c, x, b], *coefs[k]) for k in range(S)]
    return tuple((parts[0][ri] + parts[1][ri]) + (parts[2][ri] + parts[3][ri]) for ri in range(2))


def inner_kernel(scal_ref, tile_ref, sides_ref, basis_ref, sigma_ref):
    fill_region(scal_ref, tile_ref, sides_ref, ROWS, HALO, None, basis_ref, sigma_ref)
    for k in range(S):
        apply_step(basis_ref, sigma_ref, k, (HALO + k + 1,), ROWS - 2 * k - 2)


def first_kernel(
    scal_ref, last_ref, first_ref, above_ref, below_ref, _, __, basis_ref, sigma_ref, gram_ref, sums_ref
):
    fill_region(scal_ref, last_ref, above_ref, HALO, 0, 0, basis_ref, sigma_ref)
    fill_region(scal_ref, first_ref, below_ref, HALO, HALO + ROWS, 2, basis_ref, sigma_ref)
    for k in range(S):
        apply_step(basis_ref, sigma_ref, k, (k + 1, HALO + ROWS - k - 1), HALO)
    gram(basis_ref, sums_ref, gram_ref)


def next_kernel(sweep, gathered_ref, old_ref, sigma_ref, *refs):
    if sweep == 1:
        basis_ref, part_ref, gram_ref, sums_ref = refs
        old_part = None
    else:
        old_part, basis_ref, part_ref, gram_ref, sums_ref = refs
    coefs = coefficients(gathered_ref)
    begin, end = S * sweep, WIDE - S * sweep

    def residual_row(x):
        for c in range(3):
            for b in range(2):
                real, imag = new_residual(old_ref, coefs, c, x, b)
                basis_ref[0, 0, c, x, b] = real
                basis_ref[0, 1, c, x, b] = imag

    def tile_row(x):
        residual_row(x)
        for c in range(3):
            for b in range(2):
                part = solution_part(old_ref, coefs, c, x, b)
                for ri in range(2):
                    value = part[ri] if old_part is None else part[ri] + old_part[ri, c, x - HALO, b]
                    part_ref[ri, c, x - HALO, b] = value

    each(begin, HALO, 4, residual_row)
    each(HALO, HALO + ROWS, 2, tile_row)
    each(HALO + ROWS, end, 4, residual_row)
    for k in range(S):
        apply_step(basis_ref, sigma_ref, k, (begin + k + 1,), end - begin - 2 * k - 2)
    gram(basis_ref, sums_ref, gram_ref)


def last_kernel(gathered_ref, old_ref, old_part, part_ref, residual_ref):
    coefs = coefficients(gathered_ref)
    own = lane_index(NZ) < 64
    order = column_order(True)

    def store(out_ref, group, blocks):
        packed = [jnp.where(own, even, roll_lanes(odd, 64)) for even, odd in blocks]
        rows = reorder(jnp.concatenate(packed, axis=0), order)
        for x in range(ROWS):
            out_ref[pl.ds(group * (NZ * ROWS) + x, NZ, stride=ROWS), :] = rows[NZ * x : NZ * x + NZ]

    def body(c, _):
        residual, part = ([[], []] for _ in range(2))
        for x in range(ROWS):
            rs = [new_residual(old_ref, coefs, c, HALO + x, b) for b in range(2)]
            ps = [solution_part(old_ref, coefs, c, HALO + x, b) for b in range(2)]
            for ri in range(2):
                residual[ri].append((rs[0][ri], rs[1][ri]))
                part[ri].append(tuple(ps[b][ri] + old_part[ri, c, x, b] for b in range(2)))
        for ri in range(2):
            store(residual_ref, 3 * ri + c, residual[ri])
            store(part_ref, 3 * ri + c, part[ri])
        return 0

    lax.fori_loop(0, 3, body, 0)


def two_sum(a, b):
    total = a + b
    other = total - a
    return total, (a - (total - other)) + (b - other)


def quick_sum(a, b):
    total = a + b
    return total, b - (total - a)


def pair_sum(a, b):
    total, error = two_sum(a[0], b[0])
    return quick_sum(total, error + (a[1] + b[1]))


def halves(a):
    scaled = a * 4097.0
    high = scaled - (scaled - a)
    return high, a - high


def two_product(a, b):
    product = a * b
    (ah, al), (bh, bl) = halves(a), halves(b)
    return product, ((ah * bh - product) + ah * bl + al * bh) + al * bl


def pair_product(a, b):
    product, error = two_product(a[0], b[0])
    return quick_sum(product, error + (a[0] * b[1] + a[1] * b[0]))


def negative(a):
    return -a[0], -a[1]


def choose(mask, a, b):
    return jnp.where(mask, a[0], b[0]), jnp.where(mask, a[1], b[1])


def all_lanes(value):
    for step in (64, 32, 16, 8, 4, 2, 1):
        value = pair_sum(value, tuple(roll_lanes(part, step) for part in value))
    return value


def all_devices(gathered_ref):
    rows = gathered_ref.shape[0] // 2
    value = two_sum(gathered_ref[:rows, :], gathered_ref[rows:, :])
    while rows > 8:
        rows = rows // 2
        value = pair_sum(tuple(v[:rows] for v in value), tuple(v[rows:] for v in value))
    step = rows // 2
    while step:
        value = pair_sum(value, tuple(pltpu.roll(v, step, 0) for v in value))
        step = step // 2
    return tuple(jnp.broadcast_to(v[:1], BLOCK) for v in value)


def constants():
    size = DEGREE + 1
    step = np.zeros((size + 1, size), np.complex128)
    for k in range(size):
        step[k, k] = complex(*CENTER)
        step[k + 1, k] = 1.0
        if k:
            step[k - 1, k] = BETA * (2 if k == 1 else 1)
    power = [np.eye(size)[0].astype(np.complex128)]
    for _ in range(S):
        power.append(step[:size] @ power[-1])
    lanes = [(a, b, 0) for a, b in BIG_PAIRS] + [(a, b, 1) for a, b in BIG_PAIRS if a != b]
    table = np.zeros((32, LANES), np.float64)
    pick_a, pick_b = np.zeros((LANES, LANES)), np.zeros((LANES, LANES))
    for lane, (a, b, imag) in enumerate(lanes):
        pick_a[a, lane] = pick_b[b, lane] = 1
        for row, (j, k) in enumerate(ALL_PAIRS):
            first = np.conj(power[j][a]) * power[k][b]
            second = np.conj(power[j][b]) * power[k][a]
            total = first if a == b else 1j * (first - second) if imag else first + second
            table[row, lane], table[16 + row, lane] = total.real, total.imag
    high = table.astype(np.float32)
    low = (table - high).astype(np.float32)
    rows = np.zeros((16, LANES), np.float32)
    for k in range(S + 1):
        rows[k, :size], rows[8 + k, :size] = power[k].real, power[k].imag
    picks = np.stack([pick_a, pick_b]).astype(jnp.bfloat16)
    select = np.zeros((2, 32, 32))
    for row, pair in enumerate(ALL_PAIRS):
        for side in range(2):
            select[side, row, pair[side]] = select[side, 16 + row, 16 + pair[side]] = 1
    return np.concatenate([high, low, rows]), picks, select.astype(jnp.bfloat16)


def pick_rows(select, value):
    first = value.astype(jnp.bfloat16)
    rest = value - first.astype(jnp.float32)
    second = rest.astype(jnp.bfloat16)
    third = (rest - second.astype(jnp.float32)).astype(jnp.bfloat16)
    parts = [jnp.dot(select, part, preferred_element_type=jnp.float32) for part in (first, second, third)]
    return (parts[0] + parts[1]) + parts[2]


def entries(rows):
    return {pair: (rows[p : p + 1], rows[16 + p : 17 + p]) for p, pair in enumerate(ALL_PAIRS)}


def both_iterations(gathered_ref, table_ref, picks_ref, select_ref):
    sums = all_devices(gathered_ref)
    lane = lane_index(1)
    four = tuple(jnp.concatenate([v] * 4, axis=0) for v in sums)
    table = table_ref[0:32, :], table_ref[32:64, :]
    second = entries(all_lanes(pair_product(table, four))[0])
    y = solve(second)
    power = [(table_ref[64 + k : 65 + k, :], table_ref[72 + k : 73 + k, :]) for k in range(S + 1)]
    residual = power[0]
    for k in range(S):
        residual = csub(residual, cmul(y[k], power[k + 1]))
    down = jnp.where(lane == 0, 2 * BETA, jnp.where(lane < DEGREE, BETA, 0.0))
    up = jnp.where((lane > 0) & (lane <= DEGREE), 1.0, 0.0)
    chain = [residual]
    for _ in range(S):
        p = chain[-1]
        side = [down * roll_lanes(v, -1) + up * roll_lanes(v, 1) for v in p]
        turned = cmul(CENTER, p)
        chain.append((turned[0] + side[0], turned[1] + side[1]))
    gap = jnp.zeros((16 - len(chain), LANES), jnp.float32)
    stack = jnp.concatenate([v[0] for v in chain] + [gap] + [v[1] for v in chain] + [gap], axis=0)
    at_a, at_b = reorder(stack, picks_ref[0]), reorder(stack, picks_ref[1])
    aj, ak = pick_rows(select_ref[0], at_a), pick_rows(select_ref[1], at_a)
    bj, bk = pick_rows(select_ref[0], at_b), pick_rows(select_ref[1], at_b)

    def product(left, right):
        (lr, li), (rr, ri) = (left[:16], left[16:]), (right[:16], right[16:])
        real = pair_sum(two_product(lr, rr), two_product(li, ri))
        return real, pair_sum(two_product(lr, ri), negative(two_product(li, rr)))

    lanes16 = lane_index(16)
    whole = len(BIG_PAIRS)
    sign = jnp.where(lanes16 <= DEGREE, 0.0, jnp.where(lanes16 < whole, 1.0, -1.0))
    first, other = product(aj, bk), product(bj, ak)
    real, imag = (pair_sum(f, (sign * o[0], sign * o[1])) for f, o in zip(first, other))
    mixed = lanes16 >= whole
    parts = choose(mixed, negative(imag), real), choose(mixed, real, imag)
    rows = tuple(jnp.concatenate([parts[0][n], parts[1][n]], axis=0) for n in range(2))
    third = entries(all_lanes(pair_product(rows, four))[0])
    z = solve(third)

    norms = jnp.sqrt(jnp.where(lane <= DEGREE, sums[0][:1], 0.0))
    sizes = [jnp.abs(v[0]) + jnp.abs(v[1]) for v in chain + power]
    sizes = jnp.concatenate([size * norms for size in sizes], axis=0)
    for step in (64, 32, 16, 8, 4, 2, 1):
        sizes = sizes + roll_lanes(sizes, step)
    spread = None
    for at, source in ((0, third), (S + 1, second)):
        for k in range(S + 1):
            size = sizes[at + k : at + k + 1]
            ratio = size * size / source[k, k][0]
            spread = ratio if spread is None else jnp.where(ratio < spread, spread, ratio)
    part = None
    for k in range(S):
        term = cmul(y[k], power[k])
        other = cmul(z[k], chain[k])
        term = (term[0] + other[0], term[1] + other[1])
        part = term if part is None else (part[0] + term[0], part[1] + term[1])
        residual = csub(residual, cmul(z[k], chain[k + 1]))
    return part, residual, spread


def packed(even, odd):
    return jnp.where(lane_index(NZ) < 64, even, roll_lanes(odd, 64))


def wide_kernel(gathered_ref, old_ref, sigma_ref, tile_ref, part_ref, gram_ref, basis_ref, acc_ref, sums_ref):
    coefs = coefficients(gathered_ref)
    begin, end = S, WIDE - S

    def residual_row(x):
        for c in range(3):
            for b in range(2):
                real, imag = new_residual(old_ref, coefs, c, x, b)
                basis_ref[0, 0, c, x, b] = real
                basis_ref[0, 1, c, x, b] = imag

    def tile_row(x):
        residual_row(x)
        for c in range(3):
            even, odd = (solution_part(old_ref, coefs, c, x, b) for b in range(2))
            for ri in range(2):
                part_ref[ri, c, x - HALO] = packed(even[ri], odd[ri])

    each(begin, HALO, 4, residual_row)
    each(HALO, HALO + ROWS, 2, tile_row)
    each(HALO + ROWS, end, 4, residual_row)
    for k in range(DEGREE):
        apply_step(basis_ref, sigma_ref, k, (begin + k + 1,), end - begin - 2 * k - 2, (k - 1, k, k + 1))
    acc_ref[...] = jnp.zeros(acc_ref.shape, jnp.float32)

    def gram_row(x, _):
        vs = []
        for k in range(DEGREE + 1):
            vs.append([[packed(basis_ref[k, ri, c, x, 0], basis_ref[k, ri, c, x, 1]) for c in range(3)] for ri in range(2)])
            for ri in range(2):
                for c in range(3):
                    tile_ref[k, ri, c, x - HALO] = vs[k][ri][c]
        at = len(BIG_PAIRS)
        for index, (j, k) in enumerate(BIG_PAIRS):
            left, right = vs[j], vs[k]
            acc_ref[index] += tree([left[0][c] * right[0][c] + left[1][c] * right[1][c] for c in range(3)])
            if j != k:
                acc_ref[at] += tree([left[0][c] * right[1][c] - left[1][c] * right[0][c] for c in range(3)])
                at += 1
        return 0

    lax.fori_loop(HALO, HALO + ROWS, gram_row, 0)
    sums_ref[...] = jnp.zeros((LANES, LANES), jnp.float32)
    for at in range(BIG_COUNT):
        sums_ref[at : at + 1, :] = jnp.sum(acc_ref[at], axis=0, keepdims=True)
    total_lanes(sums_ref, gram_ref)


def end_kernel(
    gathered_ref, table_ref, picks_ref, select_ref, tile_ref, old_part, part_ref, residual_ref, again_ref, coef_ref
):
    part, residual, spread = both_iterations(gathered_ref, table_ref, picks_ref, select_ref)
    again_ref[0, 0] = jnp.where(spread[0, 0] < SPREAD_MAX, 0, 1)
    for a in range(DEGREE + 1):
        for n, value in enumerate(part + residual):
            coef_ref[4 * a + n] = jnp.broadcast_to(value[:, a : a + 1], BLOCK)
    order = column_order(True)

    def body(c, _):
        sums = [[] for _ in range(4)]
        for x in range(ROWS):
            totals = [old_part[0, c, x], old_part[1, c, x], None, None]
            for a in range(DEGREE + 1):
                real, imag = tile_ref[a, 0, c, x], tile_ref[a, 1, c, x]
                for out in range(2):
                    if out == 0 and a == DEGREE:
                        continue
                    term = turn(real, imag, coef_ref[4 * a + 2 * out], coef_ref[4 * a + 2 * out + 1])
                    for ri in range(2):
                        old = totals[2 * out + ri]
                        totals[2 * out + ri] = term[ri] if old is None else old + term[ri]
            for n in range(4):
                sums[n].append(totals[n])
        for n in range(4):
            rows = reorder(jnp.concatenate(sums[n], axis=0), order)
            out_ref = residual_ref if n >= 2 else part_ref
            group = 3 * (n % 2) + c
            for x in range(ROWS):
                out_ref[pl.ds(group * (NZ * ROWS) + x, NZ, stride=ROWS), :] = rows[NZ * x : NZ * x + NZ]
        return 0

    lax.fori_loop(0, 3, body, 0)


BASIS = (S + 1, 2, 3, WIDE, 2) + BLOCK
PART = (2, 3, ROWS, 2) + BLOCK


def run_inner(*operands):
    return pl.pallas_call(
        inner_kernel,
        out_shape=(vmem(BASIS), vmem((3, WIDE, 2) + BLOCK)),
        in_specs=[SMEM] + [VMEM] * 2,
        out_specs=(VMEM,) * 2,
        compiler_params=pltpu.CompilerParams(vmem_limit_bytes=LIMIT),
        cost_estimate=pl.CostEstimate(flops=8_000_000, bytes_accessed=8_000_000, transcendentals=0),
        name="inner_part",
    )(*operands)


def run_first(peers, *operands):
    return pl.pallas_call(
        first_kernel,
        out_shape=(
            vmem(BASIS), vmem((3, WIDE, 2) + BLOCK), jax.ShapeDtypeStruct((peers, LANES), jnp.float32)
        ),
        in_specs=[SMEM] + [VMEM] * 6,
        out_specs=(VMEM,) * 3,
        scratch_shapes=[vmem((LANES, LANES))],
        input_output_aliases={5: 0, 6: 1},
        compiler_params=pltpu.CompilerParams(vmem_limit_bytes=LIMIT),
        name="first_sweep",
    )(*operands)


def run_next(peers, sweep, *operands):
    return pl.pallas_call(
        functools.partial(next_kernel, sweep),
        out_shape=(vmem(BASIS), vmem(PART), jax.ShapeDtypeStruct((peers, LANES), jnp.float32)),
        in_specs=[VMEM] * len(operands),
        out_specs=(VMEM,) * 3,
        scratch_shapes=[vmem((LANES, LANES))],
        compiler_params=pltpu.CompilerParams(vmem_limit_bytes=LIMIT),
        name="second_sweep" if sweep == 1 else "third_sweep",
    )(*operands)


def run_wide(peers, *operands):
    return pl.pallas_call(
        wide_kernel,
        out_shape=(
            vmem((DEGREE + 1, 2, 3, ROWS) + BLOCK),
            vmem((2, 3, ROWS) + BLOCK),
            jax.ShapeDtypeStruct((peers, LANES), jnp.float32),
        ),
        in_specs=[VMEM] * 3,
        out_specs=(VMEM,) * 3,
        scratch_shapes=[
            vmem((DEGREE + 1, 2, 3, WIDE, 2) + BLOCK), vmem((BIG_COUNT,) + BLOCK), vmem((LANES, LANES))
        ],
        compiler_params=pltpu.CompilerParams(vmem_limit_bytes=24 * 1024 * 1024),
        name="second_third_basis",
    )(*operands)


def run_end(*operands):
    shape = jax.ShapeDtypeStruct((6 * NZ * ROWS, LANES), jnp.float32)
    tables = [jnp.asarray(table) for table in constants()]
    part, residual, again = pl.pallas_call(
        end_kernel,
        out_shape=(shape, shape, jax.ShapeDtypeStruct((1, 1), jnp.int32)),
        in_specs=[VMEM] * 6,
        out_specs=(VMEM, VMEM, SMEM),
        scratch_shapes=[vmem((4 * (DEGREE + 1),) + BLOCK)],
        compiler_params=pltpu.CompilerParams(vmem_limit_bytes=LIMIT),
        name="second_third_update",
    )(operands[0], *tables, *operands[1:])
    return tuple(out.reshape(2, 3, NZ, ROWS, LANES) for out in (part, residual)) + (again[0, 0],)


def run_last(*operands):
    shape = jax.ShapeDtypeStruct((6 * NZ * ROWS, LANES), jnp.float32)
    outs = pl.pallas_call(
        last_kernel,
        out_shape=(shape, shape),
        in_specs=[VMEM] * 3,
        out_specs=(VMEM,) * 2,
        compiler_params=pltpu.CompilerParams(vmem_limit_bytes=LIMIT),
        name="last_update",
    )(*operands)
    return tuple(out.reshape(2, 3, NZ, ROWS, LANES) for out in outs)


def spread(partial):
    return lax.all_to_all(partial, ("gx", "gy"), 0, 0, tiled=True)


def phases(bloch_index):
    theta = 2.0 * math.pi * bloch_index.astype(jnp.float32) / bloch_steps
    rows = []
    for axis, angle in (("gx", theta[0]), ("gy", theta[1])):
        spot, peers = lax.axis_index(axis), lax.axis_size(axis)
        cosine, sine = jnp.cos(angle), jnp.sin(angle)
        rows += [jnp.where(spot == 0, cosine, 1.0), jnp.where(spot == 0, -sine, 0.0)]
        rows += [jnp.where(spot == peers - 1, cosine, 1.0), jnp.where(spot == peers - 1, sine, 0.0)]
    return jnp.stack(rows)


def ring(axis, step):
    peers = lax.axis_size(axis)
    return [(i, (i + step) % peers) for i in range(peers)]


def first_sweep(right_side, conductivity, bloch_index):
    peers = lax.axis_size("gx") * lax.axis_size("gy")
    scal = phases(bloch_index)
    tile, last, first, strips = pack_messages(right_side, conductivity)
    before = lax.ppermute(strips, "gy", ring("gy", 1))
    after = lax.ppermute(strips, "gy", ring("gy", -1))
    above = lax.ppermute(last, "gx", ring("gx", 1))
    below = lax.ppermute(first, "gx", ring("gx", -1))
    from_left = (lax.broadcasted_iota(jnp.int32, strips.shape, 3) // 8) % 2 == 1
    sides = jnp.where(from_left, before, after)
    corners_above = lax.ppermute(sides[:, 1:], "gx", ring("gx", 1))
    corners_below = lax.ppermute(sides[:, :-1], "gx", ring("gx", -1))
    inner = run_inner(scal, tile, sides)
    basis, sigma, partial = run_first(peers, scal, above, below, corners_above, corners_below, *inner)
    return peers, basis, sigma, spread(partial)


def three_reductions(*operands):
    peers, basis, sigma, gathered = first_sweep(*operands)
    basis, part, partial = run_next(peers, 1, gathered, basis, sigma)
    basis, part, partial = run_next(peers, 2, spread(partial), basis, sigma, part)
    return run_last(spread(partial), basis, part)


def two_reductions(*operands):
    peers, basis, sigma, gathered = first_sweep(*operands)
    tile, part, partial = run_wide(peers, gathered, basis, sigma)
    return run_end(spread(partial), tile, part)


def shards(*operands):
    part, residual, again = two_reductions(*operands)

    def repeat(_):
        return (jnp.int32(0),) + three_reductions(*operands)

    return lax.while_loop(lambda state: state[0] > 0, repeat, (again, part, residual))[1:]


def solution(mesh):
    in_specs = (P(None, None, None, "gx", "gy"), P(None, None, "gx", "gy"), P())
    out_specs = (P(None, None, None, "gx", "gy"), P(None, None, None, "gx", "gy"))
    return jax.shard_map(shards, mesh=mesh, in_specs=in_specs, out_specs=out_specs, check_vma=False)
```

```python
import functools
import math

import jax
import jax.numpy as jnp
import numpy as np
from jax import lax
from jax.experimental import pallas as pl
from jax.experimental.pallas import tpu as pltpu
from jax.sharding import PartitionSpec as P

S = 4
NZ = 8
ROWS = 16
LANES = 128
HALO = 12
NEAR = 4
FAR = HALO - NEAR
WIDE = ROWS + 2 * HALO

shift_real = 0.5
level_step = 0.4
basis_scale = 16.0
ridge_share = 0.001
bloch_steps = 16.0


VMEM = pl.BlockSpec(memory_space=pltpu.VMEM)
SMEM = pl.BlockSpec(memory_space=pltpu.SMEM)
HBM = pl.BlockSpec(memory_space=pltpu.HBM)
LIMIT = 16 * 1024 * 1024
PAIRS = [(j, k) for j in range(S + 1) for k in range(j, S + 1) if k > 0]
BLOCK = (NZ, LANES)

DEGREE = 2 * S
CENTER = (6.25, 0.75)
BETA = 8.5
SPREAD_MAX = 3.0e4
BIG_PAIRS = [(a, a) for a in range(DEGREE + 1)] + [(a, b) for a in range(DEGREE + 1) for b in range(a + 1, DEGREE + 1)]
BIG_COUNT = len(BIG_PAIRS) + DEGREE * (DEGREE + 1) // 2
ALL_PAIRS = [(0, 0)] + PAIRS


def vmem(shape):
    return pltpu.VMEM(shape, jnp.float32)


def lane_index(rows):
    return lax.broadcasted_iota(jnp.int32, (rows, LANES), 1)


def roll_lanes(value, shift):
    shift = shift % LANES
    return pltpu.roll(value, shift, 1) if shift else value


def column_order(transposed):
    row = lax.broadcasted_iota(jnp.int32, (LANES, LANES), 0)
    lane = lax.broadcasted_iota(jnp.int32, (LANES, LANES), 1)
    column, place = (lane, row) if transposed else (row, lane)
    wanted = jnp.where(place < 64, 2 * place, 2 * place - (LANES - 1))
    return jnp.where(column == wanted, 1.0, 0.0).astype(jnp.bfloat16)


def reorder(value, order):
    first = value.astype(jnp.bfloat16)
    rest = value - first.astype(jnp.float32)
    second = rest.astype(jnp.bfloat16)
    third = (rest - second.astype(jnp.float32)).astype(jnp.bfloat16)
    parts = [jnp.dot(part, order, preferred_element_type=jnp.float32) for part in (first, second, third)]
    return (parts[0] + parts[1]) + parts[2]


def pack_kernel(rs_hbm, cond_hbm, tile_ref, last_ref, first_ref, strip_ref, rs_ref, cond_ref, sems):
    copies = [
        pltpu.make_async_copy(rs_hbm, rs_ref, sems.at[0]),
        pltpu.make_async_copy(cond_hbm, cond_ref, sems.at[1]),
    ]
    for copy in copies:
        copy.start()
    order = column_order(False)
    eighth = (lane_index(NZ) // 8) % 8

    def pack(source, offset):
        def body(group):
            start = (group - offset) * (NZ * ROWS)
            rows = [source[pl.ds(start + x, NZ, stride=ROWS), :] for x in range(ROWS)]
            mixed = reorder(jnp.concatenate(rows, axis=0), order)
            rows = [mixed[NZ * x : NZ * x + NZ] for x in range(ROWS)]
            for x in range(ROWS):
                tile_ref[group, x] = rows[x]
                if x >= ROWS - NEAR:
                    last_ref[group, x - (ROWS - NEAR)] = rows[x]
                if x < NEAR:
                    first_ref[group, x] = rows[x]
            for four in range(ROWS // 4):
                strip = None
                for j in range(4):
                    moved = roll_lanes(rows[4 * four + j], 64 + 16 * j)
                    if strip is None:
                        strip = moved
                    else:
                        strip = jnp.where((eighth == 2 * j) | (eighth == (7 + 2 * j) % 8), moved, strip)
                strip_ref[group, four] = strip

        return body

    copies[0].wait()
    each(0, 6, 3, pack(rs_ref, 0))
    copies[1].wait()
    each(6, 9, 3, pack(cond_ref, 6))


def pack_messages(right_side, conductivity):
    edge = vmem((9, NEAR) + BLOCK)
    return pl.pallas_call(
        pack_kernel,
        out_shape=(vmem((9, ROWS) + BLOCK), edge, edge, vmem((9, ROWS // 4) + BLOCK)),
        in_specs=[HBM, HBM],
        out_specs=(VMEM,) * 4,
        scratch_shapes=[vmem((6 * NZ * ROWS, LANES)), vmem((3 * NZ * ROWS, LANES)), pltpu.SemaphoreType.DMA((2,))],
        compiler_params=pltpu.CompilerParams(vmem_limit_bytes=LIMIT),
        name="pack_messages",
    )(right_side.reshape(6 * NZ * ROWS, LANES), conductivity.reshape(3 * NZ * ROWS, LANES))


def each(begin, end, size, body):
    def block(step, _):
        for spot in range(size):
            body(begin + step * size + spot)
        return 0

    lax.fori_loop(0, (end - begin) // size, block, 0)


def turn(real, imag, cosine, sine):
    return real * cosine - imag * sine, real * sine + imag * cosine


def fill_region(scal_ref, rows_ref, strips_ref, at, count, base, turned, basis_ref, sigma_ref):
    lanes = lane_index(NZ)
    own = lanes < 64
    cosine = jnp.where(own, 1.0, jnp.where(lanes < 96, scal_ref[6], scal_ref[4]))
    sine = jnp.where(own, 0.0, jnp.where(lanes < 96, scal_ref[7], scal_ref[5]))
    if turned is not None:
        cosine, sine = turn(cosine, sine, scal_ref[turned], scal_ref[turned + 1])

    def body(four):
        for comp in range(3):
            for j in range(4):
                x = 4 * four + j

                def pair(group):
                    row = rows_ref[group, x]
                    side = roll_lanes(strips_ref[group, at + four], -16 * j)
                    return jnp.where(own, row, side), roll_lanes(jnp.where(own, side, row), 64)

                real, imag, sigma = pair(comp), pair(comp + 3), pair(comp + 6)
                for b in range(2):
                    new_real, new_imag = turn(real[b], imag[b], cosine, sine)
                    basis_ref[0, 0, comp, base + x, b] = new_real
                    basis_ref[0, 1, comp, base + x, b] = new_imag
                    sigma_ref[comp, base + x, b] = level_step * sigma[b]

    each(0, count // 4, 1, body)


def minus(a, b):
    return a[0] - b[0], a[1] - b[1]


def apply_step(basis_ref, sigma_ref, k, starts, count, slots=None):
    before, here, there = (None, k, k + 1) if slots is None else slots
    beta = 0.0 if k == 0 else 2 * BETA if k == 1 else BETA
    layer = lax.broadcasted_iota(jnp.int32, BLOCK, 0)
    top, bottom = layer == NZ - 1, layer == 0
    zero = jnp.zeros(BLOCK, jnp.float32)

    def ahead_z(pair):
        return tuple(jnp.where(top, zero, pltpu.roll(v, NZ - 1, 0)) - v for v in pair)

    def back_z(pair):
        return tuple(jnp.where(bottom, zero, pltpu.roll(v, 1, 0)) - v for v in pair)

    def ahead_y(pair):
        return pair[1] - pair[0], roll_lanes(pair[0], -1) - pair[1]

    def back_y(pair):
        return roll_lanes(pair[1], 1) - pair[0], pair[0] - pair[1]

    def load(ri, c, x):
        return basis_ref[here, ri, c, x, 0], basis_ref[here, ri, c, x, 1]

    def curls(ri, x):
        ex, ey, ez = (load(ri, c, x) for c in range(3))
        hy = minus(ahead_z(ex), minus(load(ri, 2, x + 1), ez))
        hz = minus(minus(load(ri, 1, x + 1), ey), ahead_y(ex))
        return ey, ez, hy, hz

    def row(x, carry):
        fresh, outs = [], []
        for ri in range(2):
            ey, ez, hy, hz = curls(ri, x)
            hx = minus(ahead_y(ez), ahead_z(ey))
            old_y, old_z = carry[2 * ri], carry[2 * ri + 1]
            outs.append(
                (
                    minus(back_z(hy), back_y(hz)),
                    minus(minus(old_z, hz), back_z(hx)),
                    minus(back_y(hx), minus(old_y, hy)),
                )
            )
            fresh += [hy, hz]
        for c in range(3):
            real, imag = load(0, c, x), load(1, c, x)
            for b in range(2):
                sigma = sigma_ref[c, x, b]
                shift = shift_real
                if slots is not None:
                    sigma, shift = sigma - CENTER[1], shift_real - CENTER[0]
                new_real = (outs[0][c][b] + shift * real[b]) - sigma * imag[b]
                new_imag = (outs[1][c][b] + shift * imag[b]) + sigma * real[b]
                if slots is not None and k > 0:
                    new_real = new_real - beta * basis_ref[before, 0, c, x, b]
                    new_imag = new_imag - beta * basis_ref[before, 1, c, x, b]
                basis_ref[there, 0, c, x, b] = new_real
                basis_ref[there, 1, c, x, b] = new_imag
        return tuple(fresh)

    size = next(n for n in (10, 14, 13, 12, 11, 9, 8, 1) if count % n == 0) if len(starts) == 1 else 4

    def body(block, carry):
        carry = list(carry)
        for spot in range(size):
            for n, start in enumerate(starts):
                carry[4 * n : 4 * n + 4] = row(start + block * size + spot, carry[4 * n : 4 * n + 4])
        return tuple(carry)

    carry = ()
    for start in starts:
        carry += curls(0, start - 1)[2:] + curls(1, start - 1)[2:]
    lax.fori_loop(0, count // size, body, carry)


def tree(values):
    while len(values) > 1:
        values = [a + b for a, b in zip(values[::2], values[1::2])] + values[len(values) // 2 * 2 :]
    return values[0]


COUNT = len(PAIRS) + S * (S + 1) // 2


def gram_rows(basis_ref, begin, end, sums):
    def body(step, sums):
        reals, imags = [[] for _ in PAIRS], [[] for _ in PAIRS]
        for c in range(3):
            for n in range(4):
                x, b = begin + 2 * step + n // 2, n % 2
                vs = [[basis_ref[k, ri, c, x, b] for ri in range(2)] for k in range(S + 1)]
                for at, (j, k) in enumerate(PAIRS):
                    reals[at].append(vs[j][0] * vs[k][0] + vs[j][1] * vs[k][1])
                    if j != k:
                        imags[at].append(vs[j][0] * vs[k][1] - vs[j][1] * vs[k][0])
        fresh = [tree(terms) for terms in reals + imags if terms]
        return tuple(total + term for total, term in zip(sums, fresh))

    return lax.fori_loop(0, (end - begin) // 2, body, tuple(sums))


def gram(sums, sums_ref, gram_ref):
    own = lane_index(1) < 64
    sums_ref[...] = jnp.zeros((LANES, LANES), jnp.float32)
    for at, total in enumerate(sums):
        sums_ref[at : at + 1, :] = jnp.where(own, jnp.sum(total, axis=0, keepdims=True), 0.0)
    total_lanes(sums_ref, gram_ref)


def total_lanes(sums_ref, gram_ref):
    gram_ref[...] = lax.dot_general(
        jnp.ones(gram_ref.shape, jnp.float32),
        sums_ref[...],
        (((1,), (1,)), ((), ())),
        precision=lax.Precision.HIGHEST,
        preferred_element_type=jnp.float32,
    )


def cmul(a, b):
    return a[0] * b[0] - a[1] * b[1], a[0] * b[1] + a[1] * b[0]


def csub(a, b):
    return a[0] - b[0], a[1] - b[1]


def conj(a):
    return a[0], -a[1]


def solve(entry):
    unscale = [basis_scale**-k for k in range(2 * S)]
    diag = [entry[k + 1, k + 1][0] * unscale[2 * k] for k in range(S)]
    extra = (ridge_share / S) * ((diag[0] + diag[1]) + (diag[2] + diag[3]))
    diag = [d + extra for d in diag]
    low = {}
    for j in range(S):
        for k in range(j + 1, S):
            real, imag = entry[j + 1, k + 1]
            low[k, j] = (real * unscale[j + k], -imag * unscale[j + k])
    load = [(entry[0, k + 1][0] * unscale[k], -entry[0, k + 1][1] * unscale[k]) for k in range(S)]
    inverse, unit = [], {}
    for k in range(S):
        inverse.append(1.0 / diag[k])
        for i in range(k + 1, S):
            unit[i, k] = (low[i, k][0] * inverse[k], low[i, k][1] * inverse[k])
        for i in range(k + 1, S):
            real, imag = low[i, k]
            diag[i] = diag[i] - (real * real + imag * imag) * inverse[k]
            for j in range(k + 1, i):
                low[i, j] = csub(low[i, j], cmul(unit[i, k], conj(low[j, k])))
            load[i] = csub(load[i], cmul(unit[i, k], load[k]))
    answer = [None] * S
    for k in reversed(range(S)):
        value = (load[k][0] * inverse[k], load[k][1] * inverse[k])
        for j in range(k + 1, S):
            value = csub(value, cmul(conj(unit[j, k]), answer[j]))
        answer[k] = value
    return [(real * unscale[k], imag * unscale[k]) for k, (real, imag) in enumerate(answer)]


def coefficients(gathered_ref):
    row = jnp.broadcast_to(jnp.sum(gathered_ref[...], axis=0, keepdims=True), BLOCK)

    def pick(at):
        return jnp.broadcast_to(row[:, at : at + 1], BLOCK)

    entry, at = {}, len(PAIRS)
    for index, (j, k) in enumerate(PAIRS):
        if j == k:
            entry[j, k] = (pick(index), None)
        else:
            entry[j, k] = (pick(index), pick(at))
            at += 1
    return [(real[0, 0], imag[0, 0]) for real, imag in solve(entry)]


def new_residual(basis_ref, coefs, c, x, b):
    real, imag = basis_ref[0, 0, c, x, b], basis_ref[0, 1, c, x, b]
    for k in range(S):
        part = turn(basis_ref[k + 1, 0, c, x, b], basis_ref[k + 1, 1, c, x, b], *coefs[k])
        real, imag = real - part[0], imag - part[1]
    return real, imag


def solution_part(basis_ref, coefs, c, x, b):
    parts = [turn(basis_ref[k, 0, c, x, b], basis_ref[k, 1, c, x, b], *coefs[k]) for k in range(S)]
    return tuple((parts[0][ri] + parts[1][ri]) + (parts[2][ri] + parts[3][ri]) for ri in range(2))


def inner_kernel(scal_ref, tile_ref, sides_ref, basis_ref, sigma_ref, sums_ref):
    fill_region(scal_ref, tile_ref, sides_ref, 0, ROWS, HALO, None, basis_ref, sigma_ref)
    for k in range(S):
        apply_step(basis_ref, sigma_ref, k, (HALO + k + 1,), ROWS - 2 * k - 2)
    sums = gram_rows(basis_ref, HALO + S, HALO + ROWS - S, [jnp.zeros(BLOCK, jnp.float32)] * COUNT)
    for at in range(COUNT):
        sums_ref[at] = sums[at]


def first_kernel(
    scal_ref, last_ref, first_ref, above_ref, below_ref, inner_ref, _, __, basis_ref, sigma_ref, gram_ref, sums_ref
):
    fill_region(scal_ref, last_ref, above_ref, 0, NEAR, FAR, 0, basis_ref, sigma_ref)
    fill_region(scal_ref, first_ref, below_ref, 0, NEAR, HALO + ROWS, 2, basis_ref, sigma_ref)
    for k in range(S):
        apply_step(basis_ref, sigma_ref, k, (FAR + k + 1, HALO + ROWS - k - 1), NEAR)
    sums = gram_rows(basis_ref, HALO, HALO + S, [inner_ref[at] for at in range(COUNT)])
    gram(gram_rows(basis_ref, HALO + ROWS - S, HALO + ROWS, sums), sums_ref, gram_ref)


def outer_part(scal_ref, above_ref, below_ref, basis_ref, sigma_ref):
    fill_region(scal_ref, above_ref, above_ref, FAR, FAR, 0, 0, basis_ref, sigma_ref)
    fill_region(scal_ref, below_ref, below_ref, FAR, FAR, WIDE - FAR, 2, basis_ref, sigma_ref)
    for k in range(S):
        apply_step(basis_ref, sigma_ref, k, (k + 1, WIDE - FAR - k - 1), FAR)


def next_kernel(sweep, gathered_ref, *refs):
    if sweep == 1:
        scal_ref, above_ref, below_ref, _, __, old_ref, sigma_ref, basis_ref, part_ref, gram_ref, sums_ref = refs
        old_part = None
        outer_part(scal_ref, above_ref, below_ref, old_ref, sigma_ref)
    else:
        old_ref, sigma_ref, old_part, basis_ref, part_ref, gram_ref, sums_ref = refs
    coefs = coefficients(gathered_ref)
    begin, end = S * sweep, WIDE - S * sweep

    def residual_row(x):
        for c in range(3):
            for b in range(2):
                real, imag = new_residual(old_ref, coefs, c, x, b)
                basis_ref[0, 0, c, x, b] = real
                basis_ref[0, 1, c, x, b] = imag

    def tile_row(x):
        residual_row(x)
        for c in range(3):
            for b in range(2):
                part = solution_part(old_ref, coefs, c, x, b)
                for ri in range(2):
                    value = part[ri] if old_part is None else part[ri] + old_part[ri, c, x - HALO, b]
                    part_ref[ri, c, x - HALO, b] = value

    each(begin, HALO, 4, residual_row)
    each(HALO, HALO + ROWS, 2, tile_row)
    each(HALO + ROWS, end, 4, residual_row)
    for k in range(S):
        apply_step(basis_ref, sigma_ref, k, (begin + k + 1,), end - begin - 2 * k - 2)
    sums = gram_rows(basis_ref, HALO, HALO + ROWS, [jnp.zeros(BLOCK, jnp.float32)] * COUNT)
    gram(sums, sums_ref, gram_ref)


def last_kernel(gathered_ref, old_ref, old_part, part_ref, residual_ref):
    coefs = coefficients(gathered_ref)
    own = lane_index(NZ) < 64
    order = column_order(True)

    def store(out_ref, group, blocks):
        packed = [jnp.where(own, even, roll_lanes(odd, 64)) for even, odd in blocks]
        rows = reorder(jnp.concatenate(packed, axis=0), order)
        for x in range(ROWS):
            out_ref[pl.ds(group * (NZ * ROWS) + x, NZ, stride=ROWS), :] = rows[NZ * x : NZ * x + NZ]

    def body(c, _):
        residual, part = ([[], []] for _ in range(2))
        for x in range(ROWS):
            rs = [new_residual(old_ref, coefs, c, HALO + x, b) for b in range(2)]
            ps = [solution_part(old_ref, coefs, c, HALO + x, b) for b in range(2)]
            for ri in range(2):
                residual[ri].append((rs[0][ri], rs[1][ri]))
                part[ri].append(tuple(ps[b][ri] + old_part[ri, c, x, b] for b in range(2)))
        for ri in range(2):
            store(residual_ref, 3 * ri + c, residual[ri])
            store(part_ref, 3 * ri + c, part[ri])
        return 0

    lax.fori_loop(0, 3, body, 0)


def two_sum(a, b):
    total = a + b
    other = total - a
    return total, (a - (total - other)) + (b - other)


def quick_sum(a, b):
    total = a + b
    return total, b - (total - a)


def pair_sum(a, b):
    total, error = two_sum(a[0], b[0])
    return quick_sum(total, error + (a[1] + b[1]))


def halves(a):
    scaled = a * 4097.0
    high = scaled - (scaled - a)
    return high, a - high


def two_product(a, b):
    product = a * b
    (ah, al), (bh, bl) = halves(a), halves(b)
    return product, ((ah * bh - product) + ah * bl + al * bh) + al * bl


def pair_product(a, b):
    product, error = two_product(a[0], b[0])
    return quick_sum(product, error + (a[0] * b[1] + a[1] * b[0]))


def negative(a):
    return -a[0], -a[1]


def choose(mask, a, b):
    return jnp.where(mask, a[0], b[0]), jnp.where(mask, a[1], b[1])


def all_lanes(value):
    for step in (64, 32, 16, 8, 4, 2, 1):
        value = pair_sum(value, tuple(roll_lanes(part, step) for part in value))
    return value


def all_devices(gathered_ref):
    rows = gathered_ref.shape[0] // 2
    value = two_sum(gathered_ref[:rows, :], gathered_ref[rows:, :])
    while rows > 8:
        rows = rows // 2
        value = pair_sum(tuple(v[:rows] for v in value), tuple(v[rows:] for v in value))
    step = rows // 2
    while step:
        value = pair_sum(value, tuple(pltpu.roll(v, step, 0) for v in value))
        step = step // 2
    return tuple(jnp.broadcast_to(v[:1], BLOCK) for v in value)


def constants():
    size = DEGREE + 1
    step = np.zeros((size + 1, size), np.complex128)
    for k in range(size):
        step[k, k] = complex(*CENTER)
        step[k + 1, k] = 1.0
        if k:
            step[k - 1, k] = BETA * (2 if k == 1 else 1)
    power = [np.eye(size)[0].astype(np.complex128)]
    for _ in range(S):
        power.append(step[:size] @ power[-1])
    lanes = [(a, b, 0) for a, b in BIG_PAIRS] + [(a, b, 1) for a, b in BIG_PAIRS if a != b]
    table = np.zeros((32, LANES), np.float64)
    pick_a, pick_b = np.zeros((LANES, LANES)), np.zeros((LANES, LANES))
    for lane, (a, b, imag) in enumerate(lanes):
        pick_a[a, lane] = pick_b[b, lane] = 1
        for row, (j, k) in enumerate(ALL_PAIRS):
            first = np.conj(power[j][a]) * power[k][b]
            second = np.conj(power[j][b]) * power[k][a]
            total = first if a == b else 1j * (first - second) if imag else first + second
            table[row, lane], table[16 + row, lane] = total.real, total.imag
    high = table.astype(np.float32)
    low = (table - high).astype(np.float32)
    rows = np.zeros((16, LANES), np.float32)
    for k in range(S + 1):
        rows[k, :size], rows[8 + k, :size] = power[k].real, power[k].imag
    picks = np.stack([pick_a, pick_b]).astype(jnp.bfloat16)
    select = np.zeros((2, 32, 32))
    for row, pair in enumerate(ALL_PAIRS):
        for side in range(2):
            select[side, row, pair[side]] = select[side, 16 + row, 16 + pair[side]] = 1
    return np.concatenate([high, low, rows]), picks, select.astype(jnp.bfloat16)


def pick_rows(select, value):
    first = value.astype(jnp.bfloat16)
    rest = value - first.astype(jnp.float32)
    second = rest.astype(jnp.bfloat16)
    third = (rest - second.astype(jnp.float32)).astype(jnp.bfloat16)
    parts = [jnp.dot(select, part, preferred_element_type=jnp.float32) for part in (first, second, third)]
    return (parts[0] + parts[1]) + parts[2]


def entries(rows):
    return {pair: (rows[p : p + 1], rows[16 + p : 17 + p]) for p, pair in enumerate(ALL_PAIRS)}


def both_iterations(gathered_ref, table_ref, picks_ref, select_ref):
    sums = all_devices(gathered_ref)
    lane = lane_index(1)
    four = tuple(jnp.concatenate([v] * 4, axis=0) for v in sums)
    table = table_ref[0:32, :], table_ref[32:64, :]
    second = entries(all_lanes(pair_product(table, four))[0])
    y = solve(second)
    power = [(table_ref[64 + k : 65 + k, :], table_ref[72 + k : 73 + k, :]) for k in range(S + 1)]
    residual = power[0]
    for k in range(S):
        residual = csub(residual, cmul(y[k], power[k + 1]))
    down = jnp.where(lane == 0, 2 * BETA, jnp.where(lane < DEGREE, BETA, 0.0))
    up = jnp.where((lane > 0) & (lane <= DEGREE), 1.0, 0.0)
    chain = [residual]
    for _ in range(S):
        p = chain[-1]
        side = [down * roll_lanes(v, -1) + up * roll_lanes(v, 1) for v in p]
        turned = cmul(CENTER, p)
        chain.append((turned[0] + side[0], turned[1] + side[1]))
    gap = jnp.zeros((16 - len(chain), LANES), jnp.float32)
    stack = jnp.concatenate([v[0] for v in chain] + [gap] + [v[1] for v in chain] + [gap], axis=0)
    at_a, at_b = reorder(stack, picks_ref[0]), reorder(stack, picks_ref[1])
    aj, ak = pick_rows(select_ref[0], at_a), pick_rows(select_ref[1], at_a)
    bj, bk = pick_rows(select_ref[0], at_b), pick_rows(select_ref[1], at_b)

    def product(left, right):
        (lr, li), (rr, ri) = (left[:16], left[16:]), (right[:16], right[16:])
        real = pair_sum(two_product(lr, rr), two_product(li, ri))
        return real, pair_sum(two_product(lr, ri), negative(two_product(li, rr)))

    lanes16 = lane_index(16)
    whole = len(BIG_PAIRS)
    sign = jnp.where(lanes16 <= DEGREE, 0.0, jnp.where(lanes16 < whole, 1.0, -1.0))
    first, other = product(aj, bk), product(bj, ak)
    real, imag = (pair_sum(f, (sign * o[0], sign * o[1])) for f, o in zip(first, other))
    mixed = lanes16 >= whole
    parts = choose(mixed, negative(imag), real), choose(mixed, real, imag)
    rows = tuple(jnp.concatenate([parts[0][n], parts[1][n]], axis=0) for n in range(2))
    third = entries(all_lanes(pair_product(rows, four))[0])
    z = solve(third)

    norms = jnp.sqrt(jnp.where(lane <= DEGREE, sums[0][:1], 0.0))
    sizes = [jnp.abs(v[0]) + jnp.abs(v[1]) for v in chain + power]
    sizes = jnp.concatenate([size * norms for size in sizes], axis=0)
    for step in (64, 32, 16, 8, 4, 2, 1):
        sizes = sizes + roll_lanes(sizes, step)
    spread = None
    for at, source in ((0, third), (S + 1, second)):
        for k in range(S + 1):
            size = sizes[at + k : at + k + 1]
            ratio = size * size / source[k, k][0]
            spread = ratio if spread is None else jnp.where(ratio < spread, spread, ratio)
    part = None
    for k in range(S):
        term = cmul(y[k], power[k])
        other = cmul(z[k], chain[k])
        term = (term[0] + other[0], term[1] + other[1])
        part = term if part is None else (part[0] + term[0], part[1] + term[1])
        residual = csub(residual, cmul(z[k], chain[k + 1]))
    return part, residual, spread


def packed(even, odd):
    return jnp.where(lane_index(NZ) < 64, even, roll_lanes(odd, 64))


def wide_kernel(
    gathered_ref, scal_ref, above_ref, below_ref, _, __,
    old_ref, sigma_ref, tile_ref, part_ref, gram_ref, basis_ref, acc_ref, sums_ref,
):
    outer_part(scal_ref, above_ref, below_ref, old_ref, sigma_ref)
    coefs = coefficients(gathered_ref)
    begin, end = S, WIDE - S

    def residual_row(x):
        for c in range(3):
            for b in range(2):
                real, imag = new_residual(old_ref, coefs, c, x, b)
                basis_ref[0, 0, c, x, b] = real
                basis_ref[0, 1, c, x, b] = imag

    def tile_row(x):
        residual_row(x)
        for c in range(3):
            even, odd = (solution_part(old_ref, coefs, c, x, b) for b in range(2))
            for ri in range(2):
                part_ref[ri, c, x - HALO] = packed(even[ri], odd[ri])

    each(begin, HALO, 4, residual_row)
    each(HALO, HALO + ROWS, 2, tile_row)
    each(HALO + ROWS, end, 4, residual_row)
    for k in range(DEGREE):
        apply_step(basis_ref, sigma_ref, k, (begin + k + 1,), end - begin - 2 * k - 2, (k - 1, k, k + 1))
    acc_ref[...] = jnp.zeros(acc_ref.shape, jnp.float32)

    def gram_row(x, _):
        for c in range(3):
            vs = []
            for k in range(DEGREE + 1):
                vs.append([packed(basis_ref[k, ri, c, x, 0], basis_ref[k, ri, c, x, 1]) for ri in range(2)])
                for ri in range(2):
                    tile_ref[k, ri, c, x - HALO] = vs[k][ri]
            at = len(BIG_PAIRS)
            for index, (j, k) in enumerate(BIG_PAIRS):
                acc_ref[index] += vs[j][0] * vs[k][0] + vs[j][1] * vs[k][1]
                if j != k:
                    acc_ref[at] += vs[j][0] * vs[k][1] - vs[j][1] * vs[k][0]
                    at += 1
        return 0

    lax.fori_loop(HALO, HALO + ROWS, gram_row, 0)
    sums_ref[...] = jnp.zeros((LANES, LANES), jnp.float32)
    for at in range(BIG_COUNT):
        sums_ref[at : at + 1, :] = jnp.sum(acc_ref[at], axis=0, keepdims=True)
    total_lanes(sums_ref, gram_ref)


def end_kernel(
    gathered_ref, table_ref, picks_ref, select_ref, tile_ref, old_part, part_ref, residual_ref, again_ref, coef_ref
):
    part, residual, spread = both_iterations(gathered_ref, table_ref, picks_ref, select_ref)
    again_ref[0, 0] = jnp.where(spread[0, 0] < SPREAD_MAX, 0, 1)
    for a in range(DEGREE + 1):
        for n, value in enumerate(part + residual):
            coef_ref[4 * a + n] = jnp.broadcast_to(value[:, a : a + 1], BLOCK)
    order = column_order(True)

    def body(c, _):
        sums = [[] for _ in range(4)]
        for x in range(ROWS):
            totals = [old_part[0, c, x], old_part[1, c, x], None, None]
            for a in range(DEGREE + 1):
                real, imag = tile_ref[a, 0, c, x], tile_ref[a, 1, c, x]
                for out in range(2):
                    if out == 0 and a == DEGREE:
                        continue
                    term = turn(real, imag, coef_ref[4 * a + 2 * out], coef_ref[4 * a + 2 * out + 1])
                    for ri in range(2):
                        old = totals[2 * out + ri]
                        totals[2 * out + ri] = term[ri] if old is None else old + term[ri]
            for n in range(4):
                sums[n].append(totals[n])
        for n in range(4):
            rows = reorder(jnp.concatenate(sums[n], axis=0), order)
            out_ref = residual_ref if n >= 2 else part_ref
            group = 3 * (n % 2) + c
            for x in range(ROWS):
                out_ref[pl.ds(group * (NZ * ROWS) + x, NZ, stride=ROWS), :] = rows[NZ * x : NZ * x + NZ]
        return 0

    lax.fori_loop(0, 3, body, 0)


BASIS = (S + 1, 2, 3, WIDE, 2) + BLOCK
SIGMA = (3, WIDE, 2) + BLOCK
PART = (2, 3, ROWS, 2) + BLOCK


def run_inner(*operands):
    return pl.pallas_call(
        inner_kernel,
        out_shape=(vmem(BASIS), vmem(SIGMA), vmem((COUNT,) + BLOCK)),
        in_specs=[SMEM] + [VMEM] * 2,
        out_specs=(VMEM,) * 3,
        compiler_params=pltpu.CompilerParams(vmem_limit_bytes=LIMIT),
        cost_estimate=pl.CostEstimate(flops=8_000_000, bytes_accessed=8_000_000, transcendentals=0),
        name="inner_part",
    )(*operands)


def run_first(peers, *operands):
    return pl.pallas_call(
        first_kernel,
        out_shape=(
            vmem(BASIS), vmem(SIGMA), jax.ShapeDtypeStruct((peers, LANES), jnp.float32)
        ),
        in_specs=[SMEM] + [VMEM] * 7,
        out_specs=(VMEM,) * 3,
        scratch_shapes=[vmem((LANES, LANES))],
        input_output_aliases={6: 0, 7: 1},
        compiler_params=pltpu.CompilerParams(vmem_limit_bytes=LIMIT),
        name="first_sweep",
    )(*operands)


def run_next(peers, sweep, *operands):
    out_shape = (vmem(BASIS), vmem(PART), jax.ShapeDtypeStruct((peers, LANES), jnp.float32))
    if sweep == 1:
        out_shape = (vmem(BASIS), vmem(SIGMA)) + out_shape
    outs = pl.pallas_call(
        functools.partial(next_kernel, sweep),
        out_shape=out_shape,
        in_specs=[VMEM, SMEM] + [VMEM] * 4 if sweep == 1 else [VMEM] * 4,
        out_specs=(VMEM,) * len(out_shape),
        scratch_shapes=[vmem((LANES, LANES))],
        input_output_aliases={4: 0, 5: 1} if sweep == 1 else {},
        compiler_params=pltpu.CompilerParams(vmem_limit_bytes=LIMIT),
        name="second_sweep" if sweep == 1 else "third_sweep",
    )(*operands)
    return outs if sweep == 1 else (None, None) + tuple(outs)


def run_wide(peers, *operands):
    return pl.pallas_call(
        wide_kernel,
        out_shape=(
            vmem(BASIS),
            vmem(SIGMA),
            vmem((DEGREE + 1, 2, 3, ROWS) + BLOCK),
            vmem((2, 3, ROWS) + BLOCK),
            jax.ShapeDtypeStruct((peers, LANES), jnp.float32),
        ),
        in_specs=[VMEM, SMEM] + [VMEM] * 4,
        out_specs=(VMEM,) * 5,
        input_output_aliases={4: 0, 5: 1},
        scratch_shapes=[
            vmem((DEGREE + 1, 2, 3, WIDE, 2) + BLOCK), vmem((BIG_COUNT,) + BLOCK), vmem((LANES, LANES))
        ],
        compiler_params=pltpu.CompilerParams(vmem_limit_bytes=24 * 1024 * 1024),
        name="second_third_basis",
    )(*operands)


def run_end(*operands):
    shape = jax.ShapeDtypeStruct((6 * NZ * ROWS, LANES), jnp.float32)
    tables = [jnp.asarray(table) for table in constants()]
    part, residual, again = pl.pallas_call(
        end_kernel,
        out_shape=(shape, shape, jax.ShapeDtypeStruct((1, 1), jnp.int32)),
        in_specs=[VMEM] * 6,
        out_specs=(VMEM, VMEM, SMEM),
        scratch_shapes=[vmem((4 * (DEGREE + 1),) + BLOCK)],
        compiler_params=pltpu.CompilerParams(vmem_limit_bytes=LIMIT),
        name="second_third_update",
    )(operands[0], *tables, *operands[1:])
    return tuple(out.reshape(2, 3, NZ, ROWS, LANES) for out in (part, residual)) + (again[0, 0],)


def run_last(*operands):
    shape = jax.ShapeDtypeStruct((6 * NZ * ROWS, LANES), jnp.float32)
    outs = pl.pallas_call(
        last_kernel,
        out_shape=(shape, shape),
        in_specs=[VMEM] * 3,
        out_specs=(VMEM,) * 2,
        compiler_params=pltpu.CompilerParams(vmem_limit_bytes=LIMIT),
        name="last_update",
    )(*operands)
    return tuple(out.reshape(2, 3, NZ, ROWS, LANES) for out in outs)


def spread(partial):
    return lax.all_to_all(partial, ("gx", "gy"), 0, 0, tiled=True)


def phases(bloch_index):
    theta = (2.0 * math.pi * bloch_index.astype(jnp.float32) / bloch_steps)[:, None]
    axis = lax.broadcasted_iota(jnp.int32, (2, 4), 0)
    place = lax.broadcasted_iota(jnp.int32, (2, 4), 1)
    spot = jnp.where(axis == 0, lax.axis_index("gx"), lax.axis_index("gy"))
    last = jnp.where(axis == 0, lax.axis_size("gx"), lax.axis_size("gy")) - 1
    at_end = spot == jnp.where(place < 2, 0, last)
    sine = jnp.where(place < 2, -jnp.sin(theta), jnp.sin(theta))
    cosine = jnp.cos(theta)
    even = place % 2 == 0
    return jnp.where(at_end, jnp.where(even, cosine, sine), jnp.where(even, 1.0, 0.0)).reshape(8)


def ring(axis, step):
    peers = lax.axis_size(axis)
    return [(i, (i + step) % peers) for i in range(peers)]


def first_sweep(right_side, conductivity, bloch_index):
    peers = lax.axis_size("gx") * lax.axis_size("gy")
    scal = phases(bloch_index)
    tile, last, first, strips = pack_messages(right_side, conductivity)
    before = lax.ppermute(strips, "gy", ring("gy", 1))
    after = lax.ppermute(strips, "gy", ring("gy", -1))
    above = lax.ppermute(last, "gx", ring("gx", 1))
    below = lax.ppermute(first, "gx", ring("gx", -1))
    from_left = (lax.broadcasted_iota(jnp.int32, strips.shape, 3) // 8) % 2 == 1
    sides = jnp.where(from_left, before, after)
    corners_above = lax.ppermute(sides[:, 3:], "gx", ring("gx", 1))
    corners_below = lax.ppermute(sides[:, :1], "gx", ring("gx", -1))
    far = jnp.concatenate([tile[:, NEAR:HALO], sides[:, 1:3]], axis=1)
    basis, sigma, inner = run_inner(scal, tile, sides)
    far, inner, above, below, corners_above, corners_below = lax.optimization_barrier(
        (far, inner, above, below, corners_above, corners_below)
    )
    far_above = lax.ppermute(far, "gx", ring("gx", 1))
    far_below = lax.ppermute(far, "gx", ring("gx", -1))
    basis, sigma, partial = run_first(peers, scal, above, below, corners_above, corners_below, inner, basis, sigma)
    return peers, (spread(partial), scal, far_above, far_below, basis, sigma)


def three_reductions(*operands):
    peers, state = first_sweep(*operands)
    _, sigma, basis, part, partial = run_next(peers, 1, *state)
    _, _, basis, part, partial = run_next(peers, 2, spread(partial), basis, sigma, part)
    return run_last(spread(partial), basis, part)


def two_reductions(*operands):
    peers, state = first_sweep(*operands)
    _, _, tile, part, partial = run_wide(peers, *state)
    return run_end(spread(partial), tile, part)


def shards(*operands):
    part, residual, again = two_reductions(*operands)

    def repeat(_):
        return (jnp.int32(0),) + three_reductions(*operands)

    return lax.while_loop(lambda state: state[0] > 0, repeat, (again, part, residual))[1:]


def solution(mesh):
    in_specs = (P(None, None, None, "gx", "gy"), P(None, None, "gx", "gy"), P())
    out_specs = (P(None, None, None, "gx", "gy"), P(None, None, None, "gx", "gy"))
    return jax.shard_map(shards, mesh=mesh, in_specs=in_specs, out_specs=out_specs, check_vma=False)
```

```python
import functools
import math

import jax
import jax.numpy as jnp
import numpy as np
from jax import lax
from jax.experimental import pallas as pl
from jax.experimental.pallas import tpu as pltpu
from jax.sharding import PartitionSpec as P

S = 4
NZ = 8
ROWS = 16
LANES = 128
HALO = 12
WIDE = ROWS + 2 * HALO

shift_real = 0.5
level_step = 0.4
basis_scale = 16.0
ridge_share = 0.001
bloch_steps = 16.0


VMEM = pl.BlockSpec(memory_space=pltpu.VMEM)
SMEM = pl.BlockSpec(memory_space=pltpu.SMEM)
HBM = pl.BlockSpec(memory_space=pltpu.HBM)
LIMIT = 16 * 1024 * 1024
PAIRS = [(j, k) for j in range(S + 1) for k in range(j, S + 1) if k > 0]
BLOCK = (NZ, LANES)

DEGREE = 2 * S
CENTER = (6.25, 0.75)
BETA = 8.5
SPREAD_MAX = 3.0e4
BIG_PAIRS = [(a, a) for a in range(DEGREE + 1)] + [(a, b) for a in range(DEGREE + 1) for b in range(a + 1, DEGREE + 1)]
BIG_COUNT = len(BIG_PAIRS) + DEGREE * (DEGREE + 1) // 2
ALL_PAIRS = [(0, 0)] + PAIRS


def vmem(shape):
    return pltpu.VMEM(shape, jnp.float32)


def lane_index(rows):
    return lax.broadcasted_iota(jnp.int32, (rows, LANES), 1)


def roll_lanes(value, shift):
    shift = shift % LANES
    return pltpu.roll(value, shift, 1) if shift else value


def column_order(transposed):
    row = lax.broadcasted_iota(jnp.int32, (LANES, LANES), 0)
    lane = lax.broadcasted_iota(jnp.int32, (LANES, LANES), 1)
    column, place = (lane, row) if transposed else (row, lane)
    wanted = jnp.where(place < 64, 2 * place, 2 * place - (LANES - 1))
    return jnp.where(column == wanted, 1.0, 0.0).astype(jnp.bfloat16)


def reorder(value, order):
    first = value.astype(jnp.bfloat16)
    rest = value - first.astype(jnp.float32)
    second = rest.astype(jnp.bfloat16)
    third = (rest - second.astype(jnp.float32)).astype(jnp.bfloat16)
    parts = [jnp.dot(part, order, preferred_element_type=jnp.float32) for part in (first, second, third)]
    return (parts[0] + parts[1]) + parts[2]


def pack_kernel(rs_hbm, cond_hbm, tile_ref, last_ref, first_ref, strip_ref, rs_ref, cond_ref, sems):
    copies = [
        pltpu.make_async_copy(rs_hbm, rs_ref, sems.at[0]),
        pltpu.make_async_copy(cond_hbm, cond_ref, sems.at[1]),
    ]
    for copy in copies:
        copy.start()
    order = column_order(False)
    eighth = (lane_index(NZ) // 8) % 8

    def pack(source, offset):
        def body(group):
            start = (group - offset) * (NZ * ROWS)
            rows = [source[pl.ds(start + x, NZ, stride=ROWS), :] for x in range(ROWS)]
            mixed = reorder(jnp.concatenate(rows, axis=0), order)
            rows = [mixed[NZ * x : NZ * x + NZ] for x in range(ROWS)]
            for x in range(ROWS):
                tile_ref[group, x] = rows[x]
                if x >= ROWS - HALO:
                    last_ref[group, x - (ROWS - HALO)] = rows[x]
                if x < HALO:
                    first_ref[group, x] = rows[x]
            for four in range(ROWS // 4):
                strip = None
                for j in range(4):
                    moved = roll_lanes(rows[4 * four + j], 64 + 16 * j)
                    if strip is None:
                        strip = moved
                    else:
                        strip = jnp.where((eighth == 2 * j) | (eighth == (7 + 2 * j) % 8), moved, strip)
                strip_ref[group, four] = strip

        return body

    copies[0].wait()
    each(0, 6, 3, pack(rs_ref, 0))
    copies[1].wait()
    each(6, 9, 3, pack(cond_ref, 6))


def pack_messages(right_side, conductivity):
    rows, edge = (9, ROWS) + BLOCK, (9, HALO) + BLOCK
    return pl.pallas_call(
        pack_kernel,
        out_shape=(vmem(rows), vmem(edge), vmem(edge), vmem((9, ROWS // 4) + BLOCK)),
        in_specs=[HBM, HBM],
        out_specs=(VMEM,) * 4,
        scratch_shapes=[vmem((6 * NZ * ROWS, LANES)), vmem((3 * NZ * ROWS, LANES)), pltpu.SemaphoreType.DMA((2,))],
        compiler_params=pltpu.CompilerParams(vmem_limit_bytes=LIMIT),
        name="pack_messages",
    )(right_side.reshape(6 * NZ * ROWS, LANES), conductivity.reshape(3 * NZ * ROWS, LANES))


def each(begin, end, size, body):
    def block(step, _):
        for spot in range(size):
            body(begin + step * size + spot)
        return 0

    lax.fori_loop(0, (end - begin) // size, block, 0)


def turn(real, imag, cosine, sine):
    return real * cosine - imag * sine, real * sine + imag * cosine


def fill_region(scal_ref, rows_ref, strips_ref, count, base, turned, basis_ref, sigma_ref):
    lanes = lane_index(NZ)
    own = lanes < 64
    cosine = jnp.where(own, 1.0, jnp.where(lanes < 96, scal_ref[6], scal_ref[4]))
    sine = jnp.where(own, 0.0, jnp.where(lanes < 96, scal_ref[7], scal_ref[5]))
    if turned is not None:
        cosine, sine = turn(cosine, sine, scal_ref[turned], scal_ref[turned + 1])

    def body(four):
        for comp in range(3):
            for j in range(4):
                x = 4 * four + j

                def pair(group):
                    row = rows_ref[group, x]
                    side = roll_lanes(strips_ref[group, four], -16 * j)
                    return jnp.where(own, row, side), roll_lanes(jnp.where(own, side, row), 64)

                real, imag, sigma = pair(comp), pair(comp + 3), pair(comp + 6)
                for b in range(2):
                    new_real, new_imag = turn(real[b], imag[b], cosine, sine)
                    basis_ref[0, 0, comp, base + x, b] = new_real
                    basis_ref[0, 1, comp, base + x, b] = new_imag
                    sigma_ref[comp, base + x, b] = level_step * sigma[b]

    each(0, count // 4, 1, body)


def minus(a, b):
    return a[0] - b[0], a[1] - b[1]


def apply_step(basis_ref, sigma_ref, k, starts, count, slots=None):
    before, here, there = (None, k, k + 1) if slots is None else slots
    beta = 0.0 if k == 0 else 2 * BETA if k == 1 else BETA
    layer = lax.broadcasted_iota(jnp.int32, BLOCK, 0)
    top, bottom = layer == NZ - 1, layer == 0
    zero = jnp.zeros(BLOCK, jnp.float32)

    def ahead_z(pair):
        return tuple(jnp.where(top, zero, pltpu.roll(v, NZ - 1, 0)) - v for v in pair)

    def back_z(pair):
        return tuple(jnp.where(bottom, zero, pltpu.roll(v, 1, 0)) - v for v in pair)

    def ahead_y(pair):
        return pair[1] - pair[0], roll_lanes(pair[0], -1) - pair[1]

    def back_y(pair):
        return roll_lanes(pair[1], 1) - pair[0], pair[0] - pair[1]

    def load(ri, c, x):
        return basis_ref[here, ri, c, x, 0], basis_ref[here, ri, c, x, 1]

    def curls(ri, x):
        ex, ey, ez = (load(ri, c, x) for c in range(3))
        hy = minus(ahead_z(ex), minus(load(ri, 2, x + 1), ez))
        hz = minus(minus(load(ri, 1, x + 1), ey), ahead_y(ex))
        return ey, ez, hy, hz

    def row(x, carry):
        fresh, outs = [], []
        for ri in range(2):
            ey, ez, hy, hz = curls(ri, x)
            hx = minus(ahead_y(ez), ahead_z(ey))
            old_y, old_z = carry[2 * ri], carry[2 * ri + 1]
            outs.append(
                (
                    minus(back_z(hy), back_y(hz)),
                    minus(minus(old_z, hz), back_z(hx)),
                    minus(back_y(hx), minus(old_y, hy)),
                )
            )
            fresh += [hy, hz]
        for c in range(3):
            real, imag = load(0, c, x), load(1, c, x)
            for b in range(2):
                sigma = sigma_ref[c, x, b]
                shift = shift_real
                if slots is not None:
                    sigma, shift = sigma - CENTER[1], shift_real - CENTER[0]
                new_real = (outs[0][c][b] + shift * real[b]) - sigma * imag[b]
                new_imag = (outs[1][c][b] + shift * imag[b]) + sigma * real[b]
                if slots is not None and k > 0:
                    new_real = new_real - beta * basis_ref[before, 0, c, x, b]
                    new_imag = new_imag - beta * basis_ref[before, 1, c, x, b]
                basis_ref[there, 0, c, x, b] = new_real
                basis_ref[there, 1, c, x, b] = new_imag
        return tuple(fresh)

    size = next(n for n in (10, 14, 13, 12, 11, 9, 8, 1) if count % n == 0) if len(starts) == 1 else 6

    def body(block, carry):
        carry = list(carry)
        for spot in range(size):
            for n, start in enumerate(starts):
                carry[4 * n : 4 * n + 4] = row(start + block * size + spot, carry[4 * n : 4 * n + 4])
        return tuple(carry)

    carry = ()
    for start in starts:
        carry += curls(0, start - 1)[2:] + curls(1, start - 1)[2:]
    lax.fori_loop(0, count // size, body, carry)


def tree(values):
    while len(values) > 1:
        values = [a + b for a, b in zip(values[::2], values[1::2])] + values[len(values) // 2 * 2 :]
    return values[0]


COUNT = len(PAIRS) + S * (S + 1) // 2


def gram_rows(basis_ref, begin, end, sums):
    def body(step, sums):
        reals, imags = [[] for _ in PAIRS], [[] for _ in PAIRS]
        for c in range(3):
            for n in range(4):
                x, b = begin + 2 * step + n // 2, n % 2
                vs = [[basis_ref[k, ri, c, x, b] for ri in range(2)] for k in range(S + 1)]
                for at, (j, k) in enumerate(PAIRS):
                    reals[at].append(vs[j][0] * vs[k][0] + vs[j][1] * vs[k][1])
                    if j != k:
                        imags[at].append(vs[j][0] * vs[k][1] - vs[j][1] * vs[k][0])
        fresh = [tree(terms) for terms in reals + imags if terms]
        return tuple(total + term for total, term in zip(sums, fresh))

    return lax.fori_loop(0, (end - begin) // 2, body, tuple(sums))


def gram(sums, sums_ref, gram_ref):
    own = lane_index(1) < 64
    sums_ref[...] = jnp.zeros((LANES, LANES), jnp.float32)
    for at, total in enumerate(sums):
        sums_ref[at : at + 1, :] = jnp.where(own, jnp.sum(total, axis=0, keepdims=True), 0.0)
    total_lanes(sums_ref, gram_ref)


def total_lanes(sums_ref, gram_ref):
    gram_ref[...] = lax.dot_general(
        jnp.ones(gram_ref.shape, jnp.float32),
        sums_ref[...],
        (((1,), (1,)), ((), ())),
        precision=lax.Precision.HIGHEST,
        preferred_element_type=jnp.float32,
    )


def cmul(a, b):
    return a[0] * b[0] - a[1] * b[1], a[0] * b[1] + a[1] * b[0]


def csub(a, b):
    return a[0] - b[0], a[1] - b[1]


def conj(a):
    return a[0], -a[1]


def solve(entry):
    unscale = [basis_scale**-k for k in range(2 * S)]
    diag = [entry[k + 1, k + 1][0] * unscale[2 * k] for k in range(S)]
    extra = (ridge_share / S) * ((diag[0] + diag[1]) + (diag[2] + diag[3]))
    diag = [d + extra for d in diag]
    low = {}
    for j in range(S):
        for k in range(j + 1, S):
            real, imag = entry[j + 1, k + 1]
            low[k, j] = (real * unscale[j + k], -imag * unscale[j + k])
    load = [(entry[0, k + 1][0] * unscale[k], -entry[0, k + 1][1] * unscale[k]) for k in range(S)]
    inverse, unit = [], {}
    for k in range(S):
        inverse.append(1.0 / diag[k])
        for i in range(k + 1, S):
            unit[i, k] = (low[i, k][0] * inverse[k], low[i, k][1] * inverse[k])
        for i in range(k + 1, S):
            real, imag = low[i, k]
            diag[i] = diag[i] - (real * real + imag * imag) * inverse[k]
            for j in range(k + 1, i):
                low[i, j] = csub(low[i, j], cmul(unit[i, k], conj(low[j, k])))
            load[i] = csub(load[i], cmul(unit[i, k], load[k]))
    answer = [None] * S
    for k in reversed(range(S)):
        value = (load[k][0] * inverse[k], load[k][1] * inverse[k])
        for j in range(k + 1, S):
            value = csub(value, cmul(conj(unit[j, k]), answer[j]))
        answer[k] = value
    return [(real * unscale[k], imag * unscale[k]) for k, (real, imag) in enumerate(answer)]


def coefficients(gathered_ref):
    row = jnp.broadcast_to(jnp.sum(gathered_ref[...], axis=0, keepdims=True), BLOCK)

    def pick(at):
        return jnp.broadcast_to(row[:, at : at + 1], BLOCK)

    entry, at = {}, len(PAIRS)
    for index, (j, k) in enumerate(PAIRS):
        if j == k:
            entry[j, k] = (pick(index), None)
        else:
            entry[j, k] = (pick(index), pick(at))
            at += 1
    return [(real[0, 0], imag[0, 0]) for real, imag in solve(entry)]


def new_residual(basis_ref, coefs, c, x, b):
    real, imag = basis_ref[0, 0, c, x, b], basis_ref[0, 1, c, x, b]
    for k in range(S):
        part = turn(basis_ref[k + 1, 0, c, x, b], basis_ref[k + 1, 1, c, x, b], *coefs[k])
        real, imag = real - part[0], imag - part[1]
    return real, imag


def solution_part(basis_ref, coefs, c, x, b):
    parts = [turn(basis_ref[k, 0, c, x, b], basis_ref[k, 1, c, x, b], *coefs[k]) for k in range(S)]
    return tuple((parts[0][ri] + parts[1][ri]) + (parts[2][ri] + parts[3][ri]) for ri in range(2))


def inner_kernel(scal_ref, tile_ref, sides_ref, basis_ref, sigma_ref, sums_ref):
    fill_region(scal_ref, tile_ref, sides_ref, ROWS, HALO, None, basis_ref, sigma_ref)
    for k in range(S):
        apply_step(basis_ref, sigma_ref, k, (HALO + k + 1,), ROWS - 2 * k - 2)
    sums = gram_rows(basis_ref, HALO + S, HALO + ROWS - S, [jnp.zeros(BLOCK, jnp.float32)] * COUNT)
    for at in range(COUNT):
        sums_ref[at] = sums[at]


def first_kernel(
    scal_ref, last_ref, first_ref, above_ref, below_ref, inner_ref, _, __, basis_ref, sigma_ref, gram_ref, sums_ref
):
    fill_region(scal_ref, last_ref, above_ref, HALO, 0, 0, basis_ref, sigma_ref)
    fill_region(scal_ref, first_ref, below_ref, HALO, HALO + ROWS, 2, basis_ref, sigma_ref)
    for k in range(S):
        apply_step(basis_ref, sigma_ref, k, (k + 1, HALO + ROWS - k - 1), HALO)
    sums = gram_rows(basis_ref, HALO, HALO + S, [inner_ref[at] for at in range(COUNT)])
    gram(gram_rows(basis_ref, HALO + ROWS - S, HALO + ROWS, sums), sums_ref, gram_ref)


def next_kernel(sweep, gathered_ref, old_ref, sigma_ref, *refs):
    if sweep == 1:
        basis_ref, part_ref, gram_ref, sums_ref = refs
        old_part = None
    else:
        old_part, basis_ref, part_ref, gram_ref, sums_ref = refs
    coefs = coefficients(gathered_ref)
    begin, end = S * sweep, WIDE - S * sweep

    def residual_row(x):
        for c in range(3):
            for b in range(2):
                real, imag = new_residual(old_ref, coefs, c, x, b)
                basis_ref[0, 0, c, x, b] = real
                basis_ref[0, 1, c, x, b] = imag

    def tile_row(x):
        residual_row(x)
        for c in range(3):
            for b in range(2):
                part = solution_part(old_ref, coefs, c, x, b)
                for ri in range(2):
                    value = part[ri] if old_part is None else part[ri] + old_part[ri, c, x - HALO, b]
                    part_ref[ri, c, x - HALO, b] = value

    each(begin, HALO, 4, residual_row)
    each(HALO, HALO + ROWS, 2, tile_row)
    each(HALO + ROWS, end, 4, residual_row)
    for k in range(S):
        apply_step(basis_ref, sigma_ref, k, (begin + k + 1,), end - begin - 2 * k - 2)
    sums = gram_rows(basis_ref, HALO, HALO + ROWS, [jnp.zeros(BLOCK, jnp.float32)] * COUNT)
    gram(sums, sums_ref, gram_ref)


def last_kernel(gathered_ref, old_ref, old_part, part_ref, residual_ref):
    coefs = coefficients(gathered_ref)
    own = lane_index(NZ) < 64
    order = column_order(True)

    def store(out_ref, group, blocks):
        packed = [jnp.where(own, even, roll_lanes(odd, 64)) for even, odd in blocks]
        rows = reorder(jnp.concatenate(packed, axis=0), order)
        for x in range(ROWS):
            out_ref[pl.ds(group * (NZ * ROWS) + x, NZ, stride=ROWS), :] = rows[NZ * x : NZ * x + NZ]

    def body(c, _):
        residual, part = ([[], []] for _ in range(2))
        for x in range(ROWS):
            rs = [new_residual(old_ref, coefs, c, HALO + x, b) for b in range(2)]
            ps = [solution_part(old_ref, coefs, c, HALO + x, b) for b in range(2)]
            for ri in range(2):
                residual[ri].append((rs[0][ri], rs[1][ri]))
                part[ri].append(tuple(ps[b][ri] + old_part[ri, c, x, b] for b in range(2)))
        for ri in range(2):
            store(residual_ref, 3 * ri + c, residual[ri])
            store(part_ref, 3 * ri + c, part[ri])
        return 0

    lax.fori_loop(0, 3, body, 0)


def two_sum(a, b):
    total = a + b
    other = total - a
    return total, (a - (total - other)) + (b - other)


def quick_sum(a, b):
    total = a + b
    return total, b - (total - a)


def pair_sum(a, b):
    total, error = two_sum(a[0], b[0])
    return quick_sum(total, error + (a[1] + b[1]))


def halves(a):
    scaled = a * 4097.0
    high = scaled - (scaled - a)
    return high, a - high


def two_product(a, b):
    product = a * b
    (ah, al), (bh, bl) = halves(a), halves(b)
    return product, ((ah * bh - product) + ah * bl + al * bh) + al * bl


def pair_product(a, b):
    product, error = two_product(a[0], b[0])
    return quick_sum(product, error + (a[0] * b[1] + a[1] * b[0]))


def negative(a):
    return -a[0], -a[1]


def choose(mask, a, b):
    return jnp.where(mask, a[0], b[0]), jnp.where(mask, a[1], b[1])


def all_lanes(value):
    for step in (64, 32, 16, 8, 4, 2, 1):
        value = pair_sum(value, tuple(roll_lanes(part, step) for part in value))
    return value


def all_devices(gathered_ref):
    rows = gathered_ref.shape[0] // 2
    value = two_sum(gathered_ref[:rows, :], gathered_ref[rows:, :])
    while rows > 8:
        rows = rows // 2
        value = pair_sum(tuple(v[:rows] for v in value), tuple(v[rows:] for v in value))
    step = rows // 2
    while step:
        value = pair_sum(value, tuple(pltpu.roll(v, step, 0) for v in value))
        step = step // 2
    return tuple(jnp.broadcast_to(v[:1], BLOCK) for v in value)


def constants():
    size = DEGREE + 1
    step = np.zeros((size + 1, size), np.complex128)
    for k in range(size):
        step[k, k] = complex(*CENTER)
        step[k + 1, k] = 1.0
        if k:
            step[k - 1, k] = BETA * (2 if k == 1 else 1)
    power = [np.eye(size)[0].astype(np.complex128)]
    for _ in range(S):
        power.append(step[:size] @ power[-1])
    lanes = [(a, b, 0) for a, b in BIG_PAIRS] + [(a, b, 1) for a, b in BIG_PAIRS if a != b]
    table = np.zeros((32, LANES), np.float64)
    pick_a, pick_b = np.zeros((LANES, LANES)), np.zeros((LANES, LANES))
    for lane, (a, b, imag) in enumerate(lanes):
        pick_a[a, lane] = pick_b[b, lane] = 1
        for row, (j, k) in enumerate(ALL_PAIRS):
            first = np.conj(power[j][a]) * power[k][b]
            second = np.conj(power[j][b]) * power[k][a]
            total = first if a == b else 1j * (first - second) if imag else first + second
            table[row, lane], table[16 + row, lane] = total.real, total.imag
    high = table.astype(np.float32)
    low = (table - high).astype(np.float32)
    rows = np.zeros((16, LANES), np.float32)
    for k in range(S + 1):
        rows[k, :size], rows[8 + k, :size] = power[k].real, power[k].imag
    picks = np.stack([pick_a, pick_b]).astype(jnp.bfloat16)
    select = np.zeros((2, 32, 32))
    for row, pair in enumerate(ALL_PAIRS):
        for side in range(2):
            select[side, row, pair[side]] = select[side, 16 + row, 16 + pair[side]] = 1
    return np.concatenate([high, low, rows]), picks, select.astype(jnp.bfloat16)


def pick_rows(select, value):
    first = value.astype(jnp.bfloat16)
    rest = value - first.astype(jnp.float32)
    second = rest.astype(jnp.bfloat16)
    third = (rest - second.astype(jnp.float32)).astype(jnp.bfloat16)
    parts = [jnp.dot(select, part, preferred_element_type=jnp.float32) for part in (first, second, third)]
    return (parts[0] + parts[1]) + parts[2]


def entries(rows):
    return {pair: (rows[p : p + 1], rows[16 + p : 17 + p]) for p, pair in enumerate(ALL_PAIRS)}


def both_iterations(gathered_ref, table_ref, picks_ref, select_ref):
    sums = all_devices(gathered_ref)
    lane = lane_index(1)
    four = tuple(jnp.concatenate([v] * 4, axis=0) for v in sums)
    table = table_ref[0:32, :], table_ref[32:64, :]
    second = entries(all_lanes(pair_product(table, four))[0])
    y = solve(second)
    power = [(table_ref[64 + k : 65 + k, :], table_ref[72 + k : 73 + k, :]) for k in range(S + 1)]
    residual = power[0]
    for k in range(S):
        residual = csub(residual, cmul(y[k], power[k + 1]))
    down = jnp.where(lane == 0, 2 * BETA, jnp.where(lane < DEGREE, BETA, 0.0))
    up = jnp.where((lane > 0) & (lane <= DEGREE), 1.0, 0.0)
    chain = [residual]
    for _ in range(S):
        p = chain[-1]
        side = [down * roll_lanes(v, -1) + up * roll_lanes(v, 1) for v in p]
        turned = cmul(CENTER, p)
        chain.append((turned[0] + side[0], turned[1] + side[1]))
    gap = jnp.zeros((16 - len(chain), LANES), jnp.float32)
    stack = jnp.concatenate([v[0] for v in chain] + [gap] + [v[1] for v in chain] + [gap], axis=0)
    at_a, at_b = reorder(stack, picks_ref[0]), reorder(stack, picks_ref[1])
    aj, ak = pick_rows(select_ref[0], at_a), pick_rows(select_ref[1], at_a)
    bj, bk = pick_rows(select_ref[0], at_b), pick_rows(select_ref[1], at_b)

    def product(left, right):
        (lr, li), (rr, ri) = (left[:16], left[16:]), (right[:16], right[16:])
        real = pair_sum(two_product(lr, rr), two_product(li, ri))
        return real, pair_sum(two_product(lr, ri), negative(two_product(li, rr)))

    lanes16 = lane_index(16)
    whole = len(BIG_PAIRS)
    sign = jnp.where(lanes16 <= DEGREE, 0.0, jnp.where(lanes16 < whole, 1.0, -1.0))
    first, other = product(aj, bk), product(bj, ak)
    real, imag = (pair_sum(f, (sign * o[0], sign * o[1])) for f, o in zip(first, other))
    mixed = lanes16 >= whole
    parts = choose(mixed, negative(imag), real), choose(mixed, real, imag)
    rows = tuple(jnp.concatenate([parts[0][n], parts[1][n]], axis=0) for n in range(2))
    third = entries(all_lanes(pair_product(rows, four))[0])
    z = solve(third)

    norms = jnp.sqrt(jnp.where(lane <= DEGREE, sums[0][:1], 0.0))
    sizes = [jnp.abs(v[0]) + jnp.abs(v[1]) for v in chain + power]
    sizes = jnp.concatenate([size * norms for size in sizes], axis=0)
    for step in (64, 32, 16, 8, 4, 2, 1):
        sizes = sizes + roll_lanes(sizes, step)
    spread = None
    for at, source in ((0, third), (S + 1, second)):
        for k in range(S + 1):
            size = sizes[at + k : at + k + 1]
            ratio = size * size / source[k, k][0]
            spread = ratio if spread is None else jnp.where(ratio < spread, spread, ratio)
    part = None
    for k in range(S):
        term = cmul(y[k], power[k])
        other = cmul(z[k], chain[k])
        term = (term[0] + other[0], term[1] + other[1])
        part = term if part is None else (part[0] + term[0], part[1] + term[1])
        residual = csub(residual, cmul(z[k], chain[k + 1]))
    return part, residual, spread


def packed(even, odd):
    return jnp.where(lane_index(NZ) < 64, even, roll_lanes(odd, 64))


def wide_kernel(gathered_ref, old_ref, sigma_ref, tile_ref, part_ref, gram_ref, basis_ref, acc_ref, sums_ref):
    coefs = coefficients(gathered_ref)
    begin, end = S, WIDE - S

    def residual_row(x):
        for c in range(3):
            for b in range(2):
                real, imag = new_residual(old_ref, coefs, c, x, b)
                basis_ref[0, 0, c, x, b] = real
                basis_ref[0, 1, c, x, b] = imag

    def tile_row(x):
        residual_row(x)
        for c in range(3):
            even, odd = (solution_part(old_ref, coefs, c, x, b) for b in range(2))
            for ri in range(2):
                part_ref[ri, c, x - HALO] = packed(even[ri], odd[ri])

    each(begin, HALO, 4, residual_row)
    each(HALO, HALO + ROWS, 2, tile_row)
    each(HALO + ROWS, end, 4, residual_row)
    for k in range(DEGREE):
        apply_step(basis_ref, sigma_ref, k, (begin + k + 1,), end - begin - 2 * k - 2, (k - 1, k, k + 1))
    acc_ref[...] = jnp.zeros(acc_ref.shape, jnp.float32)

    def gram_row(x, _):
        for c in range(3):
            vs = []
            for k in range(DEGREE + 1):
                vs.append([packed(basis_ref[k, ri, c, x, 0], basis_ref[k, ri, c, x, 1]) for ri in range(2)])
                for ri in range(2):
                    tile_ref[k, ri, c, x - HALO] = vs[k][ri]
            at = len(BIG_PAIRS)
            for index, (j, k) in enumerate(BIG_PAIRS):
                acc_ref[index] += vs[j][0] * vs[k][0] + vs[j][1] * vs[k][1]
                if j != k:
                    acc_ref[at] += vs[j][0] * vs[k][1] - vs[j][1] * vs[k][0]
                    at += 1
        return 0

    lax.fori_loop(HALO, HALO + ROWS, gram_row, 0)
    sums_ref[...] = jnp.zeros((LANES, LANES), jnp.float32)
    for at in range(BIG_COUNT):
        sums_ref[at : at + 1, :] = jnp.sum(acc_ref[at], axis=0, keepdims=True)
    total_lanes(sums_ref, gram_ref)


def end_kernel(
    gathered_ref, table_ref, picks_ref, select_ref, tile_ref, old_part, part_ref, residual_ref, again_ref, coef_ref
):
    part, residual, spread = both_iterations(gathered_ref, table_ref, picks_ref, select_ref)
    again_ref[0, 0] = jnp.where(spread[0, 0] < SPREAD_MAX, 0, 1)
    for a in range(DEGREE + 1):
        for n, value in enumerate(part + residual):
            coef_ref[4 * a + n] = jnp.broadcast_to(value[:, a : a + 1], BLOCK)
    order = column_order(True)

    def body(c, _):
        sums = [[] for _ in range(4)]
        for x in range(ROWS):
            totals = [old_part[0, c, x], old_part[1, c, x], None, None]
            for a in range(DEGREE + 1):
                real, imag = tile_ref[a, 0, c, x], tile_ref[a, 1, c, x]
                for out in range(2):
                    if out == 0 and a == DEGREE:
                        continue
                    term = turn(real, imag, coef_ref[4 * a + 2 * out], coef_ref[4 * a + 2 * out + 1])
                    for ri in range(2):
                        old = totals[2 * out + ri]
                        totals[2 * out + ri] = term[ri] if old is None else old + term[ri]
            for n in range(4):
                sums[n].append(totals[n])
        for n in range(4):
            rows = reorder(jnp.concatenate(sums[n], axis=0), order)
            out_ref = residual_ref if n >= 2 else part_ref
            group = 3 * (n % 2) + c
            for x in range(ROWS):
                out_ref[pl.ds(group * (NZ * ROWS) + x, NZ, stride=ROWS), :] = rows[NZ * x : NZ * x + NZ]
        return 0

    lax.fori_loop(0, 3, body, 0)


BASIS = (S + 1, 2, 3, WIDE, 2) + BLOCK
PART = (2, 3, ROWS, 2) + BLOCK


def run_inner(*operands):
    return pl.pallas_call(
        inner_kernel,
        out_shape=(vmem(BASIS), vmem((3, WIDE, 2) + BLOCK), vmem((COUNT,) + BLOCK)),
        in_specs=[SMEM] + [VMEM] * 2,
        out_specs=(VMEM,) * 3,
        compiler_params=pltpu.CompilerParams(vmem_limit_bytes=LIMIT),
        cost_estimate=pl.CostEstimate(flops=8_000_000, bytes_accessed=8_000_000, transcendentals=0),
        name="inner_part",
    )(*operands)


def run_first(peers, *operands):
    return pl.pallas_call(
        first_kernel,
        out_shape=(
            vmem(BASIS), vmem((3, WIDE, 2) + BLOCK), jax.ShapeDtypeStruct((peers, LANES), jnp.float32)
        ),
        in_specs=[SMEM] + [VMEM] * 7,
        out_specs=(VMEM,) * 3,
        scratch_shapes=[vmem((LANES, LANES))],
        input_output_aliases={6: 0, 7: 1},
        compiler_params=pltpu.CompilerParams(vmem_limit_bytes=LIMIT),
        name="first_sweep",
    )(*operands)


def run_next(peers, sweep, *operands):
    return pl.pallas_call(
        functools.partial(next_kernel, sweep),
        out_shape=(vmem(BASIS), vmem(PART), jax.ShapeDtypeStruct((peers, LANES), jnp.float32)),
        in_specs=[VMEM] * len(operands),
        out_specs=(VMEM,) * 3,
        scratch_shapes=[vmem((LANES, LANES))],
        compiler_params=pltpu.CompilerParams(vmem_limit_bytes=LIMIT),
        name="second_sweep" if sweep == 1 else "third_sweep",
    )(*operands)


def run_wide(peers, *operands):
    return pl.pallas_call(
        wide_kernel,
        out_shape=(
            vmem((DEGREE + 1, 2, 3, ROWS) + BLOCK),
            vmem((2, 3, ROWS) + BLOCK),
            jax.ShapeDtypeStruct((peers, LANES), jnp.float32),
        ),
        in_specs=[VMEM] * 3,
        out_specs=(VMEM,) * 3,
        scratch_shapes=[
            vmem((DEGREE + 1, 2, 3, WIDE, 2) + BLOCK), vmem((BIG_COUNT,) + BLOCK), vmem((LANES, LANES))
        ],
        compiler_params=pltpu.CompilerParams(vmem_limit_bytes=24 * 1024 * 1024),
        name="second_third_basis",
    )(*operands)


def run_end(*operands):
    shape = jax.ShapeDtypeStruct((6 * NZ * ROWS, LANES), jnp.float32)
    tables = [jnp.asarray(table) for table in constants()]
    part, residual, again = pl.pallas_call(
        end_kernel,
        out_shape=(shape, shape, jax.ShapeDtypeStruct((1, 1), jnp.int32)),
        in_specs=[VMEM] * 6,
        out_specs=(VMEM, VMEM, SMEM),
        scratch_shapes=[vmem((4 * (DEGREE + 1),) + BLOCK)],
        compiler_params=pltpu.CompilerParams(vmem_limit_bytes=LIMIT),
        name="second_third_update",
    )(operands[0], *tables, *operands[1:])
    return tuple(out.reshape(2, 3, NZ, ROWS, LANES) for out in (part, residual)) + (again[0, 0],)


def run_last(*operands):
    shape = jax.ShapeDtypeStruct((6 * NZ * ROWS, LANES), jnp.float32)
    outs = pl.pallas_call(
        last_kernel,
        out_shape=(shape, shape),
        in_specs=[VMEM] * 3,
        out_specs=(VMEM,) * 2,
        compiler_params=pltpu.CompilerParams(vmem_limit_bytes=LIMIT),
        name="last_update",
    )(*operands)
    return tuple(out.reshape(2, 3, NZ, ROWS, LANES) for out in outs)


def spread(partial):
    return lax.all_to_all(partial, ("gx", "gy"), 0, 0, tiled=True)


def phases(bloch_index):
    theta = (2.0 * math.pi * bloch_index.astype(jnp.float32) / bloch_steps)[:, None]
    axis = lax.broadcasted_iota(jnp.int32, (2, 4), 0)
    place = lax.broadcasted_iota(jnp.int32, (2, 4), 1)
    spot = jnp.where(axis == 0, lax.axis_index("gx"), lax.axis_index("gy"))
    last = jnp.where(axis == 0, lax.axis_size("gx"), lax.axis_size("gy")) - 1
    at_end = spot == jnp.where(place < 2, 0, last)
    sine = jnp.where(place < 2, -jnp.sin(theta), jnp.sin(theta))
    cosine = jnp.cos(theta)
    even = place % 2 == 0
    return jnp.where(at_end, jnp.where(even, cosine, sine), jnp.where(even, 1.0, 0.0)).reshape(8)


def ring(axis, step):
    peers = lax.axis_size(axis)
    return [(i, (i + step) % peers) for i in range(peers)]


def first_sweep(right_side, conductivity, bloch_index):
    peers = lax.axis_size("gx") * lax.axis_size("gy")
    scal = phases(bloch_index)
    tile, last, first, strips = pack_messages(right_side, conductivity)
    before = lax.ppermute(strips, "gy", ring("gy", 1))
    after = lax.ppermute(strips, "gy", ring("gy", -1))
    above = lax.ppermute(last, "gx", ring("gx", 1))
    below = lax.ppermute(first, "gx", ring("gx", -1))
    from_left = (lax.broadcasted_iota(jnp.int32, strips.shape, 3) // 8) % 2 == 1
    sides = jnp.where(from_left, before, after)
    corners_above = lax.ppermute(sides[:, 1:], "gx", ring("gx", 1))
    corners_below = lax.ppermute(sides[:, :-1], "gx", ring("gx", -1))
    basis, sigma, inner = run_inner(scal, tile, sides)
    basis, sigma, partial = run_first(peers, scal, above, below, corners_above, corners_below, inner, basis, sigma)
    return peers, basis, sigma, spread(partial)


def three_reductions(*operands):
    peers, basis, sigma, gathered = first_sweep(*operands)
    basis, part, partial = run_next(peers, 1, gathered, basis, sigma)
    basis, part, partial = run_next(peers, 2, spread(partial), basis, sigma, part)
    return run_last(spread(partial), basis, part)


def two_reductions(*operands):
    peers, basis, sigma, gathered = first_sweep(*operands)
    tile, part, partial = run_wide(peers, gathered, basis, sigma)
    return run_end(spread(partial), tile, part)


def shards(*operands):
    part, residual, again = two_reductions(*operands)

    def repeat(_):
        return (jnp.int32(0),) + three_reductions(*operands)

    return lax.while_loop(lambda state: state[0] > 0, repeat, (again, part, residual))[1:]


def solution(mesh):
    in_specs = (P(None, None, None, "gx", "gy"), P(None, None, "gx", "gy"), P())
    out_specs = (P(None, None, None, "gx", "gy"), P(None, None, None, "gx", "gy"))
    return jax.shard_map(shards, mesh=mesh, in_specs=in_specs, out_specs=out_specs, check_vma=False)
```
